256 devices in a mesh: blk: 8 (over x, y_lo), grp: 32 (over z, y_hi, core).
Axes of the slice: x: 4, y: 4 (y_hi: 2, y_lo: 2; y = y_hi * 2 + y_lo), z: 8, core: 2. Of those that a mesh axis runs over, the one named last changes fastest.
Arguments:
- features: bfloat16 [65536, 256], P(('blk', 'grp')), may hold values from -6 to 6
- blocks: bfloat16 [8, 32, 8, 24, 128, 128], P('blk', 'grp'), may hold values from -1.5 to 1.5
- block_pos: int32 [8, 32, 8, 24], P('blk', 'grp'), may hold values from 0 to 127
- counts: int32 [8, 32, 8], P('blk', 'grp'), may hold values from 1 to 24, as said below
- degree: int32 [65536], P(('blk', 'grp')), may hold values from 8 to 64
- w_self: bfloat16 [256, 256], replicated, may hold values from -0.375 to 0.375
- w_neigh: bfloat16 [256, 256], replicated, may hold values from -0.375 to 0.375
- cotangent: bfloat16 [65536, 256], P(('blk', 'grp')), may hold values from -6 to 6
Outputs:
- out: bfloat16 [65536, 256], P(('blk', 'grp'))
- grad_x: bfloat16 [65536, 256], P(('blk', 'grp'))
- grad_self: float32 [256, 256], replicated
- grad_neigh: float32 [256, 256], replicated
The draws below stay inside these ranges and needn't reach their ends.
Inputs may be any that keep to these rules, and one draw needn't show every extreme that they name: `counts`: every list holds at least one live block; on every device some list is full with 24 live blocks, and lists differ by up to a factor of eight in their live blocks. `block_pos`: positions may repeat inside a list; blocks of repeated positions add.
All inputs are finite; a program needn't handle non-finite values.
Results may differ from the reference program's by a relative error of at most 0.025.
Values may be sent and summed in bfloat16 or wider, within the bound.
No kernel may reach another device: no remote copies, remote signals or barrier semaphores. Data moves between devices by JAX's collectives and lax.ppermute only.
A program may use at most 128 MiB of HBM per device.

```python
import math
import jax
import jax.numpy as jnp
from jax import lax

F = 256
TILE = 128
ROWS_DEV = 256
MAXB = 24
SLAB = 8192
NODES = 65536
PLACES = 128
N_BLK = 8
N_GRP = 32


def draw_counts(key, part):
    key = jax.random.fold_in(key, 7)
    level_key, full_key = jax.random.split(key)
    levels = jax.random.randint(level_key, (N_BLK, N_GRP, N_BLK), 0, 4)
    shrunk = jnp.maximum(jnp.right_shift(jnp.int32(MAXB), levels.astype(jnp.int32)), 1)
    full_list = jax.random.randint(full_key, (N_BLK, N_GRP, 1), 0, N_BLK)
    offsets = jnp.arange(N_BLK, dtype=jnp.int32)[None, None, :]
    return jnp.where(offsets == full_list, MAXB, shrunk).astype(jnp.int32)


def plant(drawn, rng, low, largest):
    longest = drawn.shape.index(max(drawn.shape))
    spots = []
    for shift in (0, 1):
        where = [jax.random.randint(jax.random.fold_in(rng, axis), (), 0, length) for axis, length in enumerate(drawn.shape)]
        where[longest] = (where[longest] + shift) % drawn.shape[longest]
        spots.append(tuple(where))
    return drawn.at[spots[0]].set(low).at[spots[1]].set(largest)


def block_levels(own_key, extent, pieces, low, high):
    level, own = 1.0, jax.random.fold_in(own_key, 6)
    for position, shards_of in pieces:
        draws = jnp.exp(jax.random.uniform(jax.random.fold_in(own, position), (shards_of,), jnp.float32, low / len(pieces), high / len(pieces)))
        level = level * jnp.repeat(draws, extent[position] // shards_of).reshape([-1 if axis == position else 1 for axis in range(len(extent))])
    return level


def noise(key, dims, scale, most, cuts=(), kind=jnp.bfloat16):
    values = jax.random.normal(key, dims, jnp.float32) * scale
    if len(cuts) > 0:
        values = block_levels(key, dims, cuts, -0.22, 0.18) * values
    return jnp.clip(values, min=-most, max=most).astype(kind)


def setup_inputs(seed: int = 0) -> dict:
    key_list = jax.random.split(jax.random.key(seed), 9)
    return {
        "features": noise(key_list[0], (NODES, F), 1.0, 6.0, ((0, 256),)),
        "blocks": noise(key_list[1], (N_BLK, N_GRP, N_BLK, MAXB, TILE, TILE), 0.25, 1.5, ((0, 8), (1, 32))),
        "block_pos": plant(jax.random.randint(key_list[2], (N_BLK, N_GRP, N_BLK, MAXB), 0, PLACES), jax.random.fold_in(key_list[2], 1), 0, PLACES - 1).astype(jnp.int32),
        "counts": draw_counts(jax.random.fold_in(key_list[8], 71), 0),
        "degree": plant(jax.random.randint(key_list[4], (NODES,), 8, 65), jax.random.fold_in(key_list[4], 1), 8, 64).astype(jnp.int32),
        "w_self": noise(key_list[5], (F, F), F ** -0.5, 0.375),
        "w_neigh": noise(key_list[6], (F, F), F ** -0.5, 0.375),
        "cotangent": noise(key_list[7], (NODES, F), 1.0, 6.0, ((0, 256),)),
    }


def slab_kernel(running, block_values, block_places, live_count, feat_piece):
    tile_size = block_values.shape[-1]
    col_count = feat_piece.shape[0] // tile_size
    col_tiles = feat_piece.reshape(col_count, tile_size, feat_piece.shape[1]).astype(jnp.float32)
    picked = col_tiles[block_places % col_count]
    products = jnp.einsum('jab,jbf->jaf', block_values.astype(jnp.float32), picked, precision=lax.Precision.HIGHEST)
    slot_ids = jnp.arange(block_places.shape[0], dtype=jnp.int32)
    products = jnp.where((slot_ids < live_count)[:, None, None], products, 0.0)
    return running.at[block_places // col_count].add(products)

def class_kernel(running, block_values, block_places, live_count, grad_tiles):
    col_count = running.shape[0]
    picked = grad_tiles[block_places // col_count].astype(jnp.float32)
    products = jnp.einsum('jab,jaf->jbf', block_values.astype(jnp.float32), picked, precision=lax.Precision.HIGHEST)
    slot_ids = jnp.arange(block_places.shape[0], dtype=jnp.int32)
    products = jnp.where((slot_ids < live_count)[:, None, None], products, 0.0)
    return running.at[block_places % col_count].add(products)

def reference(features, blocks, block_pos, counts, degree, w_self, w_neigh, cotangent):
    feat_width = features.shape[1]
    col_count = ROWS_DEV // TILE
    tile_rows = SLAB // TILE
    device_total = N_BLK * N_GRP

    def forward_device(device, summed):
        device = jnp.asarray(device).astype(jnp.int32)
        cycle_pos = device // N_GRP
        group_pos = device % N_GRP

        def per_list(offset, running):
            offset = jnp.asarray(offset).astype(jnp.int32)
            source = (cycle_pos - offset) % N_BLK * N_GRP + group_pos
            feat_piece = lax.dynamic_slice_in_dim(features, (source * ROWS_DEV).astype(jnp.int32), ROWS_DEV, 0)
            return slab_kernel(running, blocks[cycle_pos, group_pos, offset], block_pos[cycle_pos, group_pos, offset], counts[cycle_pos, group_pos, offset], feat_piece)
        running = lax.fori_loop(0, N_BLK, per_list, jnp.zeros((tile_rows, TILE, feat_width), jnp.float32))
        rounded = running.astype(jnp.bfloat16).astype(jnp.float32)
        slab_start = (cycle_pos * SLAB).astype(jnp.int32)
        current = lax.dynamic_slice_in_dim(summed, slab_start, SLAB, 0)
        return lax.dynamic_update_slice_in_dim(summed, current + rounded.reshape(SLAB, feat_width), slab_start, 0)
    summed = lax.fori_loop(0, device_total, forward_device, jnp.zeros((NODES, feat_width), jnp.float32))
    scale_deg = degree.astype(jnp.float32)[:, None]
    mean_feats = (summed / scale_deg).astype(jnp.bfloat16)
    pre_act = jnp.dot(features, w_self, preferred_element_type=jnp.float32) + jnp.dot(mean_feats, w_neigh, preferred_element_type=jnp.float32)
    out = jax.nn.silu(pre_act).astype(jnp.bfloat16)
    sigma = jax.nn.sigmoid(pre_act)
    grad_pre = (cotangent.astype(jnp.float32) * sigma * (1.0 + pre_act * (1.0 - sigma))).astype(jnp.bfloat16)
    grad_slab = (jnp.dot(grad_pre, w_neigh.T, preferred_element_type=jnp.float32) / scale_deg).astype(jnp.bfloat16)

    def backward_device(device, back_sum):
        device = jnp.asarray(device).astype(jnp.int32)
        cycle_pos = device // N_GRP
        group_pos = device % N_GRP
        grad_tiles = lax.dynamic_slice_in_dim(grad_slab, (cycle_pos * SLAB).astype(jnp.int32), SLAB, 0).reshape(tile_rows, TILE, feat_width)

        def per_list(offset, running_sum):
            offset = jnp.asarray(offset).astype(jnp.int32)
            target = (cycle_pos - offset) % N_BLK * N_GRP + group_pos
            empty = jnp.zeros((col_count, TILE, feat_width), jnp.float32)
            part_sum = class_kernel(empty, blocks[cycle_pos, group_pos, offset], block_pos[cycle_pos, group_pos, offset], counts[cycle_pos, group_pos, offset], grad_tiles)
            target_start = (target * ROWS_DEV).astype(jnp.int32)
            current = lax.dynamic_slice_in_dim(running_sum, target_start, ROWS_DEV, 0)
            return lax.dynamic_update_slice_in_dim(running_sum, current + part_sum.reshape(ROWS_DEV, feat_width), target_start, 0)
        return lax.fori_loop(0, N_BLK, per_list, back_sum)
    back_sum = lax.fori_loop(0, device_total, backward_device, jnp.zeros((NODES, feat_width), jnp.float32))
    grad_x = (jnp.dot(grad_pre, w_self.T, preferred_element_type=jnp.float32) + back_sum).astype(jnp.bfloat16)
    norm_scale = 1.0 / math.sqrt(NODES)
    grad_self = jnp.dot(features.T, grad_pre, preferred_element_type=jnp.float32) * norm_scale
    grad_neigh = jnp.dot(mean_feats.T, grad_pre, preferred_element_type=jnp.float32) * norm_scale
    return (out, grad_x, grad_self, grad_neigh)
```

```python
import math

import jax
import jax.numpy as jnp
from jax import lax
from jax.experimental import pallas as pl
from jax.experimental.pallas import tpu as pltpu
from jax.sharding import PartitionSpec as P

BF16 = jnp.bfloat16
F32 = jnp.float32
GROUP = 4
MIB = 1 << 20
SMEM = pl.BlockSpec(memory_space=pltpu.SMEM)
VMEM = pl.BlockSpec(memory_space=pltpu.VMEM)
ANY = pl.BlockSpec(memory_space=pl.ANY)

RING = 8


def along_grp(x, where):
    def target(i):
        z, y, c = where(i // 4, i // 2 % 2, i % 2)
        return z % RING * 4 + y * 2 + c

    return lax.ppermute(x, "grp", [(i, target(i)) for i in range(4 * RING)])


def other_core(x):
    return along_grp(x, lambda z, y, c: (z, y, 1 - c))


def other_y(x):
    return along_grp(x, lambda z, y, c: (z, 1 - y, c))


def along_z(x, distance):
    return along_grp(x, lambda z, y, c: (z + distance, y, c))


def flip_z(x, bit):
    return along_grp(x, lambda z, y, c: (z ^ bit, y, c))


def along_blk(x, distance):
    n = lax.axis_size("blk")
    return lax.ppermute(x, "blk", [(i, (i + distance) % n) for i in range(n)])


def flip_blk(x, bit):
    n = lax.axis_size("blk")
    return lax.ppermute(x, "blk", [(i, i ^ bit) for i in range(n)])


def chunk_of(me, order, same_y, same_core):
    z, y, c = me // 4, me // 2 % 2, me % 2
    z = lax.rem(z + order + RING, RING)
    y = y if same_y else 1 - y
    c = c if same_core else 1 - c
    return z * 4 + y * 2 + c


def placed(block, col, live):
    zero = jnp.zeros_like(block)
    left = jnp.where(jnp.logical_and(live, col == 0), block, zero)
    right = jnp.where(jnp.logical_and(live, col == 1), block, zero)
    return left, right


def slab_kernel(me_ref, pos_ref, counts_ref, blocks_ref, *refs):
    feats, (send_y, send_k, keep_y, keep_k, acc, held, sems) = refs[:8], refs[8:]
    lists, slots = pos_ref.shape
    copies = [
        pltpu.make_async_copy(blocks_ref.at[k], held.at[k], sems.at[k]) for k in range(lists)
    ]
    for copy in copies:
        copy.start()

    def clear(i, _):
        acc[i] = jnp.zeros(acc.shape[1:], F32)
        return 0

    lax.fori_loop(0, acc.shape[0], clear, 0)
    for k in range(lists):
        copies[k].wait()
        live = counts_ref[k]
        feat = feats[k][...]

        def step(s, _, k=k, live=live, feat=feat):
            rows, places = [], []
            for u in range(GROUP):
                j = s * GROUP + u
                p = pos_ref[k, j]
                left, right = placed(held[k, j], p % 2, j < live)
                rows.append(jnp.concatenate([left, right], axis=1))
                places.append(p // 2)
            products = jnp.dot(jnp.concatenate(rows, axis=0), feat, preferred_element_type=F32)
            tile = rows[0].shape[0]
            for u in range(GROUP):
                acc[places[u]] += products[u * tile : (u + 1) * tile]
            return 0

        lax.fori_loop(0, (live + GROUP - 1) // GROUP, step, 0)
    me = me_ref[0]
    tile = acc.shape[1]
    for out, same_y, same_core in (
        (send_y, False, False),
        (send_k, True, False),
        (keep_y, False, True),
        (keep_k, True, True),
    ):

        def write(i, _, out=out, same_y=same_y, same_core=same_core):
            chunk = chunk_of(me, i, same_y, same_core)
            for half in range(2):
                start = pl.multiple_of((i * 2 + half) * tile, tile)
                out[pl.ds(start, tile), :] = acc[chunk * 2 + half].astype(BF16)
            return 0

        lax.fori_loop(0, RING, write, 0)


def slab_sums(me, block_pos, counts, blocks, feats):
    lists, slots, tile, _ = blocks.shape
    rows, width = feats[0].shape
    quarter = jax.ShapeDtypeStruct((RING * rows, width), BF16)
    return pl.pallas_call(
        slab_kernel,
        out_shape=(quarter,) * 4,
        in_specs=[SMEM, SMEM, SMEM, ANY] + [VMEM] * lists,
        out_specs=(VMEM,) * 4,
        scratch_shapes=[
            pltpu.VMEM((4 * RING * rows // tile, tile, width), F32),
            pltpu.VMEM(blocks.shape, BF16),
            pltpu.SemaphoreType.DMA((lists,)),
        ],
        compiler_params=pltpu.CompilerParams(vmem_limit_bytes=28 * MIB),
        cost_estimate=pl.CostEstimate(
            flops=4 * lists * slots * tile * tile * width,
            bytes_accessed=14 * MIB,
            transcendentals=0,
        ),
        name="slab_sums",
    )(me, block_pos, counts, blocks, *feats)


def mid_kernel(refs_in, refs_out):
    feats, cotangent, degree, w_self, w_neigh, parts = refs_in
    out, grad_slab, grad_self, local_self, local_neigh = refs_out
    deg = degree[...]
    summed = parts[0][...].astype(F32)
    for part in parts[1:]:
        summed = summed + part[...].astype(F32)
    mean = (summed / deg).astype(BF16)
    x, ws, wn = feats[...], w_self[...], w_neigh[...]
    pre = jnp.dot(x, ws, preferred_element_type=F32) + jnp.dot(mean, wn, preferred_element_type=F32)
    sigma = jax.nn.sigmoid(pre)
    out[...] = (pre * sigma).astype(BF16)
    grad = (cotangent[...].astype(F32) * sigma * (1.0 + pre * (1.0 - sigma))).astype(BF16)
    transposed = (((1,), (1,)), ((), ()))
    back = lax.dot_general(grad, wn, transposed, preferred_element_type=F32)
    grad_slab[...] = (back / deg).astype(BF16)
    grad_self[...] = lax.dot_general(grad, ws, transposed, preferred_element_type=F32)
    over_rows = (((0,), (0,)), ((), ()))
    local_self[...] = lax.dot_general(x, grad, over_rows, preferred_element_type=F32).astype(BF16)
    local_neigh[...] = lax.dot_general(mean, grad, over_rows, preferred_element_type=F32).astype(
        BF16
    )


def middle(feats, cotangent, degree, w_self, w_neigh, parts):
    rows, width = feats.shape

    def kernel(*refs):
        mid_kernel((*refs[:5], refs[5 : 5 + len(parts)]), refs[5 + len(parts) :])

    low, wide = jax.ShapeDtypeStruct((rows, width), BF16), jax.ShapeDtypeStruct((rows, width), F32)
    square = jax.ShapeDtypeStruct((width, width), BF16)
    return pl.pallas_call(
        kernel,
        out_shape=(low, low, wide, square, square),
        in_specs=[VMEM] * (5 + len(parts)),
        out_specs=(VMEM,) * 5,
        compiler_params=pltpu.CompilerParams(vmem_limit_bytes=16 * MIB),
        cost_estimate=pl.CostEstimate(
            flops=12 * rows * width * width, bytes_accessed=4 * MIB, transcendentals=rows * width
        ),
        name="middle",
    )(feats, cotangent, degree, w_self, w_neigh, *parts)


def class_kernel(me_ref, pos_ref, counts_ref, blocks_ref, *refs):
    lists, slots = pos_ref.shape
    pieces, (other, far), outs = refs[:RING], refs[RING : RING + 2], refs[RING + 2 : RING + 2 + lists]
    grads, held, sems = refs[RING + 2 + lists :]
    copies = [
        pltpu.make_async_copy(blocks_ref.at[k], held.at[k], sems.at[k]) for k in range(lists)
    ]
    for copy in copies:
        copy.start()
    me = me_ref[0]
    rows = pieces[0].shape[0]
    tile = grads.shape[1]

    def put(chunk, value):
        for half in range(2):
            grads[chunk * 2 + half] = value[half * tile : (half + 1) * tile]

    for i in range(RING):
        put(chunk_of(me, -i, True, True), pieces[i][...])
    for source, first, same_y, same_core in (
        (other, 0, False, True),
        (far, 0, True, False),
        (far, RING, False, False),
    ):

        def place(i, _, source=source, first=first, same_y=same_y, same_core=same_core):
            start = pl.multiple_of((first + i) * rows, rows)
            put(chunk_of(me, -i, same_y, same_core), source[pl.ds(start, rows), :])
            return 0

        lax.fori_loop(0, RING, place, 0)
    for k in range(lists):
        copies[k].wait()
        live = counts_ref[k]

        def step(s, total, k=k, live=live):
            cols, picked = [], []
            for u in range(GROUP):
                j = s * GROUP + u
                p = pos_ref[k, j]
                top, bottom = placed(held[k, j].T, p % 2, j < live)
                cols.append(jnp.concatenate([top, bottom], axis=0))
                picked.append(grads[p // 2])
            return total + jnp.dot(
                jnp.concatenate(cols, axis=1),
                jnp.concatenate(picked, axis=0),
                preferred_element_type=F32,
            )

        outs[k][...] = lax.fori_loop(
            0, (live + GROUP - 1) // GROUP, step, jnp.zeros(outs[k].shape, F32)
        ).astype(outs[k].dtype)


def class_sums(me, block_pos, counts, blocks, pieces, other, far):
    lists, slots, tile, _ = blocks.shape
    rows, width = pieces[0].shape
    return pl.pallas_call(
        class_kernel,
        out_shape=[jax.ShapeDtypeStruct((rows, width), BF16)] * lists,
        in_specs=[SMEM, SMEM, SMEM, ANY] + [VMEM] * (RING + 2),
        out_specs=[VMEM] * lists,
        scratch_shapes=[
            pltpu.VMEM((4 * RING * rows // tile, tile, width), BF16),
            pltpu.VMEM(blocks.shape, BF16),
            pltpu.SemaphoreType.DMA((lists,)),
        ],
        compiler_params=pltpu.CompilerParams(vmem_limit_bytes=28 * MIB),
        cost_estimate=pl.CostEstimate(
            flops=4 * lists * slots * tile * tile * width,
            bytes_accessed=14 * MIB,
            transcendentals=0,
        ),
        name="class_sums",
    )(me, block_pos, counts, blocks, *pieces, other, far)


def added(*terms):
    total = terms[0].astype(F32)
    for term in terms[1:]:
        total = total + term.astype(F32)
    return total.astype(BF16)


def per_device(features, blocks, block_pos, counts, degree, w_self, w_neigh, cotangent):
    cycle_size = lax.axis_size("blk")
    group_size = lax.axis_size("grp")
    rows, width = features.shape
    place = lax.axis_index("grp").astype(jnp.int32)
    me = place.reshape(1)
    block_values, block_places, live_counts = blocks[0, 0], block_pos[0, 0], counts[0, 0]

    feats = [features] + [along_blk(features, k) for k in range(1, cycle_size)]
    send_y, send_k, keep_y, keep_k = slab_sums(me, block_places, live_counts, block_values, feats)
    y_sum = added(keep_y, other_core(send_y))
    k_recv = other_core(send_k)
    y_recv = other_y(y_sum)

    def z_part(i):
        at = slice(i * rows, (i + 1) * rows)
        return added(keep_k[at], k_recv[at], y_recv[at])

    parts = [z_part(0)] + [along_z(z_part(i), i) for i in range(1, RING)]
    scale_deg = degree.astype(F32)[:, None]
    out, grad_slab, grad_self, local_self, local_neigh = middle(
        features, cotangent, scale_deg, w_self, w_neigh, parts
    )

    pieces = [grad_slab] + [along_z(grad_slab, i) for i in range(1, RING)]
    own = jnp.concatenate(pieces, axis=0)
    other = other_y(own)
    far = other_core(jnp.concatenate([own, other], axis=0))
    terms = class_sums(me, block_places, live_counts, block_values, pieces, other, far)
    sums = [terms[0]] + [along_blk(terms[k], -k) for k in range(1, cycle_size)]
    back_sum = grad_self
    for term in sums:
        back_sum = back_sum + term.astype(F32)
    grad_x = back_sum.astype(BF16)

    first = place % 2 == 0
    total = added(
        jnp.where(first, local_self, local_neigh),
        other_core(jnp.where(first, local_neigh, local_self)),
    )
    for bit in (1, 2, 4):
        total = added(total, flip_z(total, bit))
    total = added(total, other_y(total))
    for bit in (1, 2, 4):
        total = added(total, flip_blk(total, bit))
    twin = other_core(total)
    norm_scale = 1.0 / math.sqrt(rows * cycle_size * group_size)
    total_self = jnp.where(first, total, twin).astype(F32) * norm_scale
    total_neigh = jnp.where(first, twin, total).astype(F32) * norm_scale
    return (out, grad_x, total_self, total_neigh)


def solution(mesh):
    in_specs = (
        P(("blk", "grp"), None),
        P("blk", "grp", None, None, None, None),
        P("blk", "grp", None, None),
        P("blk", "grp", None),
        P(("blk", "grp")),
        P(),
        P(),
        P(("blk", "grp"), None),
    )
    out_specs = (P(("blk", "grp"), None), P(("blk", "grp"), None), P(), P())
    return jax.shard_map(
        per_device, mesh=mesh, in_specs=in_specs, out_specs=out_specs, check_vma=False
    )
```

```python
import math

import jax
import jax.numpy as jnp
from jax import lax
from jax.experimental import pallas as pl
from jax.experimental.pallas import tpu as pltpu
from jax.sharding import PartitionSpec as P

BF16 = jnp.bfloat16
F32 = jnp.float32
GROUP = 4
MIB = 1 << 20
SMEM = pl.BlockSpec(memory_space=pltpu.SMEM)
VMEM = pl.BlockSpec(memory_space=pltpu.VMEM)
KERNEL_VMEM = 24 * MIB
SLAB_STEPS = ((1, 2, 3, 4), (5, 6, 7))
CLASS_STEPS = ((7, 6, 5, 4), (3, 2, 1), (0,))

RING = 8


def along_grp(x, where):
    def target(i):
        z, y, c = where(i // 4, i // 2 % 2, i % 2)
        return z % RING * 4 + y * 2 + c

    return lax.ppermute(x, "grp", [(i, target(i)) for i in range(4 * RING)])


def other_core(x):
    return along_grp(x, lambda z, y, c: (z, y, 1 - c))


def other_y(x):
    return along_grp(x, lambda z, y, c: (z, 1 - y, c))


def along_z(x, distance):
    return along_grp(x, lambda z, y, c: (z + distance, y, c))


def flip_z(x, bit):
    return along_grp(x, lambda z, y, c: (z ^ bit, y, c))


def along_blk(x, distance):
    n = lax.axis_size("blk")
    return lax.ppermute(x, "blk", [(i, (i + distance) % n) for i in range(n)])


def flip_blk(x, bit):
    n = lax.axis_size("blk")
    return lax.ppermute(x, "blk", [(i, i ^ bit) for i in range(n)])


def chunk_of(me, order, same_y, same_core):
    z, y, c = me // 4, me // 2 % 2, me % 2
    z = lax.rem(z + order + RING, RING)
    y = y if same_y else 1 - y
    c = c if same_core else 1 - c
    return z * 4 + y * 2 + c


def placed(block, col, live):
    zero = jnp.zeros_like(block)
    left = jnp.where(jnp.logical_and(live, col == 0), block, zero)
    right = jnp.where(jnp.logical_and(live, col == 1), block, zero)
    return left, right


def slab_lists(lists, pos_ref, counts_ref, blocks_ref, feats, acc):
    for k, feat_ref in zip(lists, feats, strict=True):
        live = counts_ref[k]
        feat = feat_ref[...]

        def step(s, _, k=k, live=live, feat=feat):
            rows, places = [], []
            for u in range(GROUP):
                j = s * GROUP + u
                p = pos_ref[k, j]
                left, right = placed(blocks_ref[k, j], p % 2, j < live)
                rows.append(jnp.concatenate([left, right], axis=1))
                places.append(p // 2)
            products = jnp.dot(jnp.concatenate(rows, axis=0), feat, preferred_element_type=F32)
            tile = rows[0].shape[0]
            for u in range(GROUP):
                acc[places[u]] += products[u * tile : (u + 1) * tile]
            return 0

        lax.fori_loop(0, (live + GROUP - 1) // GROUP, step, 0)


def slab_cost(lists, slots, tile, width):
    return pl.CostEstimate(
        flops=4 * len(lists) * slots * tile * tile * width,
        bytes_accessed=MIB * len(lists),
        transcendentals=0,
    )


def slab_sums(lists, block_pos, counts, blocks, feats, acc=None):
    _, slots, tile, _ = blocks.shape
    rows, width = feats[0].shape
    shape = jax.ShapeDtypeStruct((4 * RING * rows // tile, tile, width), F32)

    def kernel(pos_ref, counts_ref, blocks_ref, *refs):
        out = refs[-1]
        if acc is None:

            def clear(i, _):
                out[i] = jnp.zeros(out.shape[1:], F32)
                return 0

            lax.fori_loop(0, out.shape[0], clear, 0)
        slab_lists(lists, pos_ref, counts_ref, blocks_ref, refs[: len(lists)], out)

    more = [] if acc is None else [acc]
    return pl.pallas_call(
        kernel,
        out_shape=shape,
        in_specs=[SMEM, SMEM, VMEM] + [VMEM] * (len(feats) + len(more)),
        out_specs=VMEM,
        input_output_aliases={3 + len(feats): 0} if more else {},
        compiler_params=pltpu.CompilerParams(vmem_limit_bytes=KERNEL_VMEM),
        cost_estimate=slab_cost(lists, slots, tile, width),
        name="slab_sums",
    )(block_pos, counts, blocks, *feats, *more)


FAR_Y = ((3, False), (-3, False), (4, False))
NEAR_Z = ((1, True), (1, False), (-1, True), (-1, False))
REST = (
    (2, False), (-2, False), (0, False),
    (3, True), (-3, True), (4, True), (2, True), (-2, True), (0, True),
)


def slab_parts(me, lists, block_pos, counts, blocks, feats, acc):
    _, slots, tile, _ = blocks.shape
    rows, width = feats[0].shape
    groups = (FAR_Y, NEAR_Z, REST)

    def kernel(me_ref, pos_ref, counts_ref, blocks_ref, *refs):
        total, outs = refs[len(lists)], refs[len(lists) + 1 :]
        slab_lists(lists, pos_ref, counts_ref, blocks_ref, refs[: len(lists)], total)
        mine = me_ref[0]
        for out, (same_core, group) in zip(
            outs, [(same, group) for same in (False, True) for group in groups], strict=True
        ):
            for i, (order, same_y) in enumerate(group):
                chunk = chunk_of(mine, order, same_y, same_core)
                for half in range(2):
                    start = (2 * i + half) * tile
                    out[start : start + tile, :] = total[chunk * 2 + half].astype(BF16)

    return pl.pallas_call(
        kernel,
        out_shape=[
            jax.ShapeDtypeStruct((len(group) * rows, width), BF16) for group in groups * 2
        ],
        in_specs=[SMEM, SMEM, SMEM, VMEM] + [VMEM] * (len(feats) + 1),
        out_specs=[VMEM] * 6,
        compiler_params=pltpu.CompilerParams(vmem_limit_bytes=KERNEL_VMEM),
        cost_estimate=slab_cost(lists, slots, tile, width),
        name="slab_parts",
    )(me, block_pos, counts, blocks, *feats, acc)


def mid_kernel(refs_in, refs_out):
    feats, cotangent, degree, w_self, w_neigh, parts = refs_in
    out, grad_slab, grad_self, local_self, local_neigh = refs_out
    deg = degree[...]
    summed = parts[0][...].astype(F32)
    for part in parts[1:]:
        summed = summed + part[...].astype(F32)
    mean = (summed / deg).astype(BF16)
    x, ws, wn = feats[...], w_self[...], w_neigh[...]
    pre = jnp.dot(x, ws, preferred_element_type=F32) + jnp.dot(mean, wn, preferred_element_type=F32)
    sigma = jax.nn.sigmoid(pre)
    out[...] = (pre * sigma).astype(BF16)
    grad = (cotangent[...].astype(F32) * sigma * (1.0 + pre * (1.0 - sigma))).astype(BF16)
    transposed = (((1,), (1,)), ((), ()))
    back = lax.dot_general(grad, wn, transposed, preferred_element_type=F32)
    grad_slab[...] = (back / deg).astype(BF16)
    grad_self[...] = lax.dot_general(grad, ws, transposed, preferred_element_type=F32)
    over_rows = (((0,), (0,)), ((), ()))
    local_self[...] = lax.dot_general(x, grad, over_rows, preferred_element_type=F32).astype(BF16)
    local_neigh[...] = lax.dot_general(mean, grad, over_rows, preferred_element_type=F32).astype(
        BF16
    )


def middle(feats, cotangent, degree, w_self, w_neigh, parts):
    rows, width = feats.shape

    def kernel(*refs):
        mid_kernel((*refs[:5], refs[5 : 5 + len(parts)]), refs[5 + len(parts) :])

    low, wide = jax.ShapeDtypeStruct((rows, width), BF16), jax.ShapeDtypeStruct((rows, width), F32)
    square = jax.ShapeDtypeStruct((width, width), BF16)
    return pl.pallas_call(
        kernel,
        out_shape=(low, low, wide, square, square),
        in_specs=[VMEM] * (5 + len(parts)),
        out_specs=(VMEM,) * 5,
        compiler_params=pltpu.CompilerParams(vmem_limit_bytes=16 * MIB),
        cost_estimate=pl.CostEstimate(
            flops=12 * rows * width * width, bytes_accessed=4 * MIB, transcendentals=rows * width
        ),
        name="middle",
    )(feats, cotangent, degree, w_self, w_neigh, *parts)


def class_cost(lists, slots, tile, width):
    return pl.CostEstimate(
        flops=4 * len(lists) * slots * tile * tile * width,
        bytes_accessed=MIB * (1 + len(lists)),
        transcendentals=0,
    )


def put(grads, chunk, value):
    tile = grads.shape[1]
    for half in range(2):
        grads[chunk * 2 + half] = value[half * tile : (half + 1) * tile]


def gathered(me, rows, pieces):
    width, tile = pieces[0][0].shape[1], rows // 2

    def kernel(me_ref, *refs):
        mine, out = me_ref[0], refs[-1]
        for ref, (_, places) in zip(refs[:-1], pieces, strict=True):
            for i, place in enumerate(places):
                put(out, chunk_of(mine, *place), ref[i * rows : (i + 1) * rows, :])

    return pl.pallas_call(
        kernel,
        out_shape=jax.ShapeDtypeStruct((4 * RING * 2, tile, width), BF16),
        in_specs=[SMEM] + [VMEM] * len(pieces),
        out_specs=VMEM,
        compiler_params=pltpu.CompilerParams(vmem_limit_bytes=KERNEL_VMEM),
        cost_estimate=pl.CostEstimate(flops=0, bytes_accessed=4 * MIB, transcendentals=0),
        name="gathered",
    )(me, *[array for array, _ in pieces])


def packed(arrays):
    starts = [0]
    for array in arrays:
        starts.append(starts[-1] + array.shape[0])

    def kernel(*refs):
        for ref, start, end in zip(refs[:-1], starts[:-1], starts[1:], strict=True):
            refs[-1][start:end, :] = ref[...]

    return pl.pallas_call(
        kernel,
        out_shape=jax.ShapeDtypeStruct((starts[-1], arrays[0].shape[1]), BF16),
        in_specs=[VMEM] * len(arrays),
        out_specs=VMEM,
        compiler_params=pltpu.CompilerParams(vmem_limit_bytes=KERNEL_VMEM),
        cost_estimate=pl.CostEstimate(flops=0, bytes_accessed=MIB, transcendentals=0),
        name="packed",
    )(*arrays)


def class_lists(lists, pos_ref, counts_ref, blocks_ref, grads, outs):
    for k, out in zip(lists, outs, strict=True):
        live = counts_ref[k]

        def step(s, total, k=k, live=live):
            cols, picked = [], []
            for u in range(GROUP):
                j = s * GROUP + u
                p = pos_ref[k, j]
                top, bottom = placed(blocks_ref[k, j].T, p % 2, j < live)
                cols.append(jnp.concatenate([top, bottom], axis=0))
                picked.append(grads[p // 2])
            return total + jnp.dot(
                jnp.concatenate(cols, axis=1),
                jnp.concatenate(picked, axis=0),
                preferred_element_type=F32,
            )

        out[...] = lax.fori_loop(
            0, (live + GROUP - 1) // GROUP, step, jnp.zeros(out.shape, F32)
        ).astype(out.dtype)


def class_sums(me, lists, block_pos, counts, blocks, grads, last=None):
    _, slots, tile, _ = blocks.shape
    width = grads.shape[2]
    rows = 2 * tile
    more = [] if last is None else [last[0]]

    def kernel(me_ref, pos_ref, counts_ref, blocks_ref, grads_ref, *refs):
        outs = refs[len(more) :]
        if more:
            grads_ref, outs = outs[0], outs[1:]
            for i, place in enumerate(last[1]):
                put(grads_ref, chunk_of(me_ref[0], *place), refs[0][i * rows : (i + 1) * rows, :])
        class_lists(lists, pos_ref, counts_ref, blocks_ref, grads_ref, outs)

    return pl.pallas_call(
        kernel,
        out_shape=[jax.ShapeDtypeStruct(grads.shape, BF16)] * len(more)
        + [jax.ShapeDtypeStruct((rows, width), BF16)] * len(lists),
        in_specs=[SMEM, SMEM, SMEM] + [VMEM] * (2 + len(more)),
        out_specs=[VMEM] * (len(more) + len(lists)),
        input_output_aliases={4: 0} if more else {},
        compiler_params=pltpu.CompilerParams(vmem_limit_bytes=KERNEL_VMEM),
        cost_estimate=class_cost(lists, slots, tile, width),
        name="class_sums",
    )(me, block_pos, counts, blocks, grads, *more)


def wide_sum(*terms):
    total = terms[0].astype(F32)
    for term in terms[1:]:
        total = total + term.astype(F32)
    return total


def added(*terms):
    return wide_sum(*terms).astype(BF16)


def half_added(total, term, first):
    rows = term.shape[0]
    edges = ((0, rows, 0), (0, 0, 0)) if first else ((rows, 0, 0), (0, 0, 0))
    return total + lax.pad(term, jnp.zeros((), term.dtype), edges).astype(F32)


def slab_reduced(rows, sent, kept):
    def at(array, first, count=1):
        return array[first * rows : (first + count) * rows]

    far = added(kept[0], other_core(sent[0]))
    far_y = other_y(far)
    near = other_core(sent[1])
    rest, more = kept[2], other_core(sent[2])
    from_behind = along_z(added(at(kept[1], 0, 2), at(near, 0, 2)), 1)
    from_ahead = along_z(added(at(kept[1], 2, 2), at(near, 2, 2)), -1)
    mid_y = other_y(added(at(rest, 0, 2), at(more, 0, 2)))
    own_y = other_y(
        added(at(rest, 2), at(more, 2), at(from_behind, 1), at(from_ahead, 1))
    )
    three_ahead = along_z(added(at(rest, 3), at(more, 3), at(far_y, 0)), 1)
    three_behind = along_z(added(at(rest, 4), at(more, 4), at(far_y, 1)), -1)
    half = rows // 2
    opposite = added(at(rest, 5), at(more, 5), at(far_y, 2))
    opposite_up = along_z(opposite[:half], 2)
    opposite_down = along_z(opposite[half:], -2)
    two_ahead = wide_sum(at(rest, 6), at(more, 6), at(mid_y, 0), three_ahead)
    two_behind = wide_sum(at(rest, 7), at(more, 7), at(mid_y, 1), three_behind)
    from_two_behind = along_z(half_added(two_ahead, opposite_up, True).astype(BF16), 2)
    from_two_ahead = along_z(half_added(two_behind, opposite_down, False).astype(BF16), -2)
    base = wide_sum(at(rest, 8), at(more, 8), at(from_behind, 0), at(from_ahead, 0))
    return [base, own_y, from_two_behind, from_two_ahead]


def slab_gathered(me, own):
    half = own.shape[0] // 2
    behind1, ahead1 = along_z(own, 1), along_z(own, -1)
    behind2, ahead2 = along_z(own, 2), along_z(own, -2)
    own_y = other_y(own)
    behind1_y, ahead1_y = along_z(own_y, 1), along_z(own_y, -1)
    behind3, ahead3 = along_z(behind2, 1), along_z(ahead2, -1)
    opposite_up, opposite_down = along_z(behind2[:half], 2), along_z(ahead2[half:], -2)
    mid_y = other_y(packed([behind2, ahead2]))
    far = packed([behind3, ahead3, opposite_up, opposite_down])
    far_y = other_y(far)
    near = packed([own, behind1, ahead1, behind2, ahead2, own_y, behind1_y, ahead1_y])
    rest = packed([mid_y, far])
    near_core, rest_core, last_core = other_core(near), other_core(rest), other_core(far_y)
    near_places = (
        (0, True), (-1, True), (1, True), (-2, True), (2, True), (0, False), (-1, False), (1, False),
    )
    mid_places = ((-2, False), (2, False))
    far_places = ((-3, True), (3, True), (4, True))
    last_places = ((-3, False), (3, False), (4, False))

    def on(places, same_core):
        return [(*place, same_core) for place in places]

    grads = gathered(
        me,
        own.shape[0],
        [
            (near, on(near_places, True)),
            (rest, on(mid_places + far_places, True)),
            (far_y, on(last_places, True)),
            (near_core, on(near_places, False)),
            (rest_core, on(mid_places + far_places, False)),
        ],
    )
    return grads, (last_core, on(last_places, False))


def weight_sums(place, local_self, local_neigh):
    first = place % 2 == 0
    total = added(
        jnp.where(first, local_self, local_neigh),
        other_core(jnp.where(first, local_neigh, local_self)),
    )
    for bit in (2, 4, 1):
        total = added(total, flip_blk(total, bit))
    total = added(total, other_y(total))
    for bit in (1, 2, 4):
        total = added(total, flip_z(total, bit))
    twin = other_core(total)
    return jnp.where(first, total, twin).astype(F32), jnp.where(first, twin, total).astype(F32)


def per_device(features, blocks, block_pos, counts, degree, w_self, w_neigh, cotangent):
    cycle_size = lax.axis_size("blk")
    group_size = lax.axis_size("grp")
    rows, width = features.shape
    place = lax.axis_index("grp").astype(jnp.int32)
    me = place.reshape(1)
    table = (block_pos[0, 0], counts[0, 0], blocks[0, 0])

    feats = [features] + [along_blk(features, k) for k in range(1, cycle_size)]
    acc = slab_sums((0,), *table, feats[:1])
    for lists in SLAB_STEPS[:-1]:
        acc = slab_sums(lists, *table, [feats[k] for k in lists], acc)
    lists = SLAB_STEPS[-1]
    shares = slab_parts(me, lists, *table, [feats[k] for k in lists], acc)
    parts = slab_reduced(rows, shares[:3], shares[3:])
    scale_deg = degree.astype(F32)[:, None]
    out, grad_slab, grad_self, local_self, local_neigh = middle(
        features, cotangent, scale_deg, w_self, w_neigh, parts
    )

    grads, last = slab_gathered(me, grad_slab)
    terms = {}
    grads, *sums = class_sums(me, CLASS_STEPS[0], *table, grads, last)
    terms.update(zip(CLASS_STEPS[0], sums, strict=True))
    for lists in CLASS_STEPS[1:]:
        sums = class_sums(me, lists, *table, grads)
        terms.update(zip(lists, sums, strict=True))
    back_sum = wide_sum(
        grad_self, terms[0], *[along_blk(terms[k], -k) for k in range(cycle_size - 1, 0, -1)]
    )
    grad_x = back_sum.astype(BF16)

    total_self, total_neigh = weight_sums(place, local_self, local_neigh)
    norm_scale = 1.0 / math.sqrt(rows * cycle_size * group_size)
    return (out, grad_x, total_self * norm_scale, total_neigh * norm_scale)


def solution(mesh):
    in_specs = (
        P(("blk", "grp"), None),
        P("blk", "grp", None, None, None, None),
        P("blk", "grp", None, None),
        P("blk", "grp", None),
        P(("blk", "grp")),
        P(),
        P(),
        P(("blk", "grp"), None),
    )
    out_specs = (P(("blk", "grp"), None), P(("blk", "grp"), None), P(), P())
    return jax.shard_map(
        per_device, mesh=mesh, in_specs=in_specs, out_specs=out_specs, check_vma=False
    )
```

```python
import math

import jax
import jax.numpy as jnp
from jax import lax
from jax.experimental import pallas as pl
from jax.experimental.pallas import tpu as pltpu
from jax.sharding import PartitionSpec as P

BF16 = jnp.bfloat16
F32 = jnp.float32
GROUP = 12
MIB = 1 << 20
SMEM = pl.BlockSpec(memory_space=pltpu.SMEM)
VMEM = pl.BlockSpec(memory_space=pltpu.VMEM)
ANY = pl.BlockSpec(memory_space=pl.ANY)
KERNEL_VMEM = 24 * MIB
COST = pl.CostEstimate(flops=1024, bytes_accessed=1024, transcendentals=0)
SLAB_STEPS = (((1, True), (3, True), (2, True), (0, False)), ((1, False), (3, False), (2, False)))
CLASS_ORDER = (2, 1, 3, 0)

RING = 8


def along_grp(x, where):
    def target(i):
        z, y, c = where(i // 4, i // 2 % 2, i % 2)
        return z % RING * 4 + y * 2 + c

    return lax.ppermute(x, "grp", [(i, target(i)) for i in range(4 * RING)])


def other_core(x):
    return along_grp(x, lambda z, y, c: (z, y, 1 - c))


def other_y(x):
    return along_grp(x, lambda z, y, c: (z, 1 - y, c))


def along_z(x, distance):
    return along_grp(x, lambda z, y, c: (z + distance, y, c))


def two_along_z(x):
    return along_grp(x, lambda z, y, c: (z + 2 - z % 2 * 4, y, c))


def flip_z(x, bit):
    return along_grp(x, lambda z, y, c: (z ^ bit, y, c))


def along_blk(x, distance):
    n = lax.axis_size("blk")
    return lax.ppermute(x, "blk", [(i, (i + distance) % n) for i in range(n)])


def flip_blk(x, bit):
    n = lax.axis_size("blk")
    return lax.ppermute(x, "blk", [(i, i ^ bit) for i in range(n)])


def chunk_of(me, order, same_y, same_core):
    z, y, c = me // 4, me // 2 % 2, me % 2
    z = lax.rem(z + order + RING, RING)
    y = y if same_y else 1 - y
    c = c if same_core else 1 - c
    return z * 4 + y * 2 + c


def placed(block, col, live):
    zero = jnp.zeros_like(block)
    left = jnp.where(jnp.logical_and(live, col == 0), block, zero)
    right = jnp.where(jnp.logical_and(live, col == 1), block, zero)
    return left, right


def slab_lists(lists, pos_ref, counts_ref, blocks_ref, feats, acc):
    for k, feat_ref in zip(lists, feats, strict=True):
        live = counts_ref[k]
        feat = feat_ref[...]

        def step(s, _, k=k, live=live, feat=feat):
            rows, places = [], []
            for u in range(GROUP):
                j = s * GROUP + u
                p = pos_ref[k, j]
                left, right = placed(blocks_ref[k, j], p % 2, j < live)
                rows.append(jnp.concatenate([left, right], axis=1))
                places.append(p // 2)
            products = jnp.dot(jnp.concatenate(rows, axis=0), feat, preferred_element_type=F32)
            tile = rows[0].shape[0]
            for u in range(GROUP):
                acc[places[u]] += products[u * tile : (u + 1) * tile]
            return 0

        lax.fori_loop(0, (live + GROUP - 1) // GROUP, step, 0)


def list_of(blk, source):
    behind, same = source
    y = blk % 2
    return (2 * behind + (0 if same else 2 * y - 1) + 8) % 8


def slab_sums(me, sources, block_pos, counts, blocks, feats, acc=None):
    _, slots, tile, _ = blocks.shape
    rows, width = feats[0].shape
    shape = jax.ShapeDtypeStruct((4 * RING * rows // tile, tile, width), F32)

    def kernel(me_ref, pos_ref, counts_ref, blocks_ref, *refs):
        out = refs[-1]
        lists = [list_of(me_ref[1], source) for source in sources]
        if acc is None:

            def clear(i, _):
                out[i] = jnp.zeros(out.shape[1:], F32)
                return 0

            lax.fori_loop(0, out.shape[0], clear, 0)
        slab_lists(lists, pos_ref, counts_ref, blocks_ref, refs[: len(sources)], out)

    more = [] if acc is None else [acc]
    return pl.pallas_call(
        kernel,
        out_shape=shape,
        in_specs=[SMEM, SMEM, SMEM, VMEM] + [VMEM] * (len(feats) + len(more)),
        out_specs=VMEM,
        input_output_aliases={4 + len(feats): 0} if more else {},
        compiler_params=pltpu.CompilerParams(vmem_limit_bytes=KERNEL_VMEM),
        cost_estimate=COST,
        name="slab_sums",
    )(me, block_pos, counts, blocks, *feats, *more)


FAR_Y = ((3, False), (-3, False), (4, False))
NEAR = ((1, True), (1, False), (-1, True), (-1, False), (2, False), (-2, False))
REST = ((3, True), (-3, True), (4, True), (2, True), (-2, True), (0, False), (0, True))


def slab_parts(me, sources, block_pos, counts, blocks, feats, acc):
    _, slots, tile, _ = blocks.shape
    rows, width = feats[0].shape
    groups = (FAR_Y, NEAR, REST)

    def kernel(me_ref, pos_ref, counts_ref, blocks_ref, *refs):
        total, outs = refs[len(sources)], refs[len(sources) + 1 :]
        lists = [list_of(me_ref[1], source) for source in sources]
        slab_lists(lists, pos_ref, counts_ref, blocks_ref, refs[: len(sources)], total)
        mine = me_ref[0]
        for out, (same_core, group) in zip(
            outs, [(same, group) for same in (False, True) for group in groups], strict=True
        ):
            for i, (order, same_y) in enumerate(group):
                chunk = chunk_of(mine, order, same_y, same_core)
                for half in range(2):
                    start = (2 * i + half) * tile
                    out[start : start + tile, :] = total[chunk * 2 + half].astype(BF16)

    return pl.pallas_call(
        kernel,
        out_shape=[
            jax.ShapeDtypeStruct((len(group) * rows, width), BF16) for group in groups * 2
        ],
        in_specs=[SMEM, SMEM, SMEM, VMEM] + [VMEM] * (len(feats) + 1),
        out_specs=[VMEM] * 6,
        compiler_params=pltpu.CompilerParams(vmem_limit_bytes=KERNEL_VMEM),
        cost_estimate=COST,
        name="slab_parts",
    )(me, block_pos, counts, blocks, *feats, acc)


def mid_kernel(refs_in, refs_out):
    me_ref, feats, cotangent, degree, w_self, w_neigh, parts = refs_in
    out, grad_slab, grad_self, mine, theirs = refs_out
    deg = degree[...]
    summed = parts[0][...].astype(F32)
    for part in parts[1:]:
        summed = summed + part[...].astype(F32)
    mean = (summed / deg).astype(BF16)
    x, ws, wn = feats[...], w_self[...], w_neigh[...]
    pre = jnp.dot(x, ws, preferred_element_type=F32) + jnp.dot(mean, wn, preferred_element_type=F32)
    sigma = jax.nn.sigmoid(pre)
    out[...] = (pre * sigma).astype(BF16)
    grad = (cotangent[...].astype(F32) * sigma * (1.0 + pre * (1.0 - sigma))).astype(BF16)
    transposed = (((1,), (1,)), ((), ()))
    back = lax.dot_general(grad, wn, transposed, preferred_element_type=F32)
    grad_slab[...] = (back / deg).astype(BF16)
    grad_self[...] = lax.dot_general(grad, ws, transposed, preferred_element_type=F32)
    over_rows = (((0,), (0,)), ((), ()))
    local_self = lax.dot_general(x, grad, over_rows, preferred_element_type=F32).astype(BF16)
    local_neigh = lax.dot_general(mean, grad, over_rows, preferred_element_type=F32).astype(BF16)
    first = me_ref[0] % 2 == 0
    mine[...] = jnp.where(first, local_self, local_neigh)
    theirs[...] = jnp.where(first, local_neigh, local_self)


def middle(me, feats, cotangent, degree, w_self, w_neigh, parts):
    rows, width = feats.shape

    def kernel(*refs):
        mid_kernel((*refs[:6], refs[6 : 6 + len(parts)]), refs[6 + len(parts) :])

    low, wide = jax.ShapeDtypeStruct((rows, width), BF16), jax.ShapeDtypeStruct((rows, width), F32)
    square = jax.ShapeDtypeStruct((width, width), BF16)
    return pl.pallas_call(
        kernel,
        out_shape=(low, low, wide, square, square),
        in_specs=[SMEM] + [VMEM] * (5 + len(parts)),
        out_specs=(VMEM,) * 5,
        compiler_params=pltpu.CompilerParams(vmem_limit_bytes=16 * MIB),
        cost_estimate=COST,
        name="middle",
    )(me, feats, cotangent, degree, w_self, w_neigh, *parts)


def put(grads, chunk, value):
    tile = grads.shape[1]
    for half in range(2):
        grads[chunk * 2 + half] = value[half * tile : (half + 1) * tile]


def gathered(me, rows, pieces, after=()):
    width, tile = pieces[0][0].shape[1], rows // 2

    def kernel(me_ref, *refs):
        mine, out = me_ref[0], refs[-1]
        for ref, (_, places) in zip(refs[: len(pieces)], pieces, strict=True):
            for i, place in enumerate(places):
                put(out, chunk_of(mine, *place), ref[i * rows : (i + 1) * rows, :])

    return pl.pallas_call(
        kernel,
        out_shape=jax.ShapeDtypeStruct((4 * RING * 2, tile, width), BF16),
        in_specs=[SMEM] + [VMEM] * len(pieces) + [ANY] * len(after),
        out_specs=VMEM,
        compiler_params=pltpu.CompilerParams(vmem_limit_bytes=KERNEL_VMEM),
        cost_estimate=COST,
        name="gathered",
    )(me, *[array for array, _ in pieces], *after)


def packed(arrays, after=()):
    starts = [0]
    for array in arrays:
        starts.append(starts[-1] + array.shape[0])

    def kernel(*refs):
        for ref, start, end in zip(refs[: len(arrays)], starts[:-1], starts[1:], strict=True):
            refs[-1][start:end, :] = ref[...]

    return pl.pallas_call(
        kernel,
        out_shape=jax.ShapeDtypeStruct((starts[-1], arrays[0].shape[1]), BF16),
        in_specs=[VMEM] * len(arrays) + [ANY] * len(after),
        out_specs=VMEM,
        compiler_params=pltpu.CompilerParams(vmem_limit_bytes=KERNEL_VMEM),
        cost_estimate=COST,
        name="packed",
    )(*arrays, *after)


def class_list(k, pos_ref, counts_ref, blocks_ref, grads, out):
    live = counts_ref[k]

    def step(s, total):
        cols, picked = [], []
        for u in range(GROUP):
            j = s * GROUP + u
            p = pos_ref[k, j]
            top, bottom = placed(blocks_ref[k, j].T, p % 2, j < live)
            cols.append(jnp.concatenate([top, bottom], axis=0))
            picked.append(grads[p // 2])
        return total + jnp.dot(
            jnp.concatenate(cols, axis=1),
            jnp.concatenate(picked, axis=0),
            preferred_element_type=F32,
        )

    out[...] = lax.fori_loop(
        0, (live + GROUP - 1) // GROUP, step, jnp.zeros(out.shape, F32)
    ).astype(out.dtype)


def class_sums(me, block_pos, counts, blocks, grads, last):
    _, slots, tile, _ = blocks.shape
    width = grads.shape[2]
    rows = 2 * tile

    def kernel(me_ref, pos_ref, counts_ref, blocks_ref, _, last_ref, grads_ref, *outs):
        for i, place in enumerate(last[1]):
            put(grads_ref, chunk_of(me_ref[0], *place), last_ref[i * rows : (i + 1) * rows, :])
        for behind, out in zip(CLASS_ORDER, outs, strict=True):
            for i, same in enumerate((True, False)):
                k = list_of(me_ref[1], (behind, same))
                view = out.at[pl.ds(i * rows, rows), :]
                class_list(k, pos_ref, counts_ref, blocks_ref, grads_ref, view)

    pair = jax.ShapeDtypeStruct((2 * rows, width), BF16)
    return pl.pallas_call(
        kernel,
        out_shape=[jax.ShapeDtypeStruct(grads.shape, BF16)] + [pair] * len(CLASS_ORDER),
        in_specs=[SMEM, SMEM, SMEM] + [VMEM] * 3,
        out_specs=[VMEM] * (1 + len(CLASS_ORDER)),
        input_output_aliases={4: 0},
        compiler_params=pltpu.CompilerParams(vmem_limit_bytes=KERNEL_VMEM),
        cost_estimate=COST,
        name="class_sums",
    )(me, block_pos, counts, blocks, grads, last[0])[1:]


def wide_sum(*terms):
    total = terms[0].astype(F32)
    for term in terms[1:]:
        total = total + term.astype(F32)
    return total


def sums(outs, after=(), me=None):
    arrays = []
    for terms in outs:
        for array, *_ in terms:
            if not any(array is other for other in arrays):
                arrays.append(array)

    def find(array):
        return next(i for i, other in enumerate(arrays) if other is array)

    scalars = [] if me is None else [me]

    def kernel(*refs):
        me_refs, refs = refs[: len(scalars)], refs[len(scalars) :]
        for out, terms in zip(refs[len(arrays) + len(after) :], outs, strict=True):
            total = None
            for array, first, count, *parity in terms:
                term = refs[find(array)][first : first + count, :].astype(F32)
                if parity:
                    mine = me_refs[0][0] // 4 % 2 == parity[0]
                    term = jnp.where(mine, term, jnp.zeros_like(term))
                total = term if total is None else total + term
            out[...] = total.astype(BF16)

    width = arrays[0].shape[1]
    return pl.pallas_call(
        kernel,
        out_shape=[jax.ShapeDtypeStruct((terms[0][2], width), BF16) for terms in outs],
        in_specs=[SMEM] * len(scalars) + [VMEM] * len(arrays) + [ANY] * len(after),
        out_specs=[VMEM] * len(outs),
        compiler_params=pltpu.CompilerParams(vmem_limit_bytes=KERNEL_VMEM),
        cost_estimate=COST,
        name="sums",
    )(*scalars, *arrays, *after)


def pair_sum(first, second, after=()):
    rows = first.shape[0]
    return sums([[(first, 0, rows), (second, 0, rows)]], after)[0]


def slab_reduced(me, rows, sent, kept):
    def at(array, first, count=1):
        return array[first * rows : (first + count) * rows]

    def both(first, count, *arrays):
        return [(array, first * rows, count * rows) for array in arrays]

    far_y = other_y(pair_sum(kept[0], other_core(sent[0])))
    near, more = kept[1], other_core(sent[1])
    ahead, behind, mid = sums([both(first, 2, near, more) for first in (0, 2, 4)])
    from_behind, from_ahead = along_z(ahead, 1), along_z(behind, -1)
    mid_y = other_y(mid)
    rest, more = kept[2], other_core(sent[2])
    ahead, behind, opposite = sums(
        [both(i, 1, rest, more, far_y) for i in range(3)], [from_behind, from_ahead]
    )
    three_ahead, three_behind = along_z(ahead, 1), along_z(behind, -1)
    opposite = two_along_z(opposite)
    one = (0, rows)
    two_ahead, two_behind = sums(
        [
            [*both(3, 1, rest, more), *both(0, 1, mid_y), (three_ahead, *one), (opposite, *one, 0)],
            [*both(4, 1, rest, more), *both(1, 1, mid_y), (three_behind, *one), (opposite, *one, 1)],
        ],
        me=me,
    )
    from_two_behind, from_two_ahead = along_z(two_ahead, 2), along_z(two_behind, -2)
    own_y = other_y(
        sums([both(5, 1, rest, more) + both(1, 1, from_behind, from_ahead)], [three_ahead])[0]
    )
    base = wide_sum(at(rest, 6), at(more, 6), at(from_behind, 0), at(from_ahead, 0))
    return [base, own_y, from_two_behind, from_two_ahead]


def slab_gathered(me, even, own, mine, theirs):
    behind2, ahead2 = along_z(own, 2), along_z(own, -2)
    own_y = other_y(own)
    behind3, ahead3 = along_z(behind2, 1), along_z(ahead2, -1)
    opposite = two_along_z(jnp.where(even, behind2, ahead2))
    total = pair_sum(mine, other_core(packed([theirs], [own_y])), [behind2, ahead2])
    mid_y = other_y(packed([behind2, ahead2], [total]))
    total = pair_sum(total, flip_blk(total, 2), [behind3, ahead3])
    far = packed([behind3, ahead3, opposite], [mid_y, total])
    far_y = other_y(far)
    total = pair_sum(total, flip_blk(total, 4), [far])
    both = packed([own, own_y], [total])
    from_behind, from_ahead = along_z(both, 1), along_z(both, -1)
    rest = packed([own, own_y, behind2, ahead2, mid_y, far])
    rest_core = other_core(rest)
    total = pair_sum(total, flip_blk(total, 1), [from_behind, from_ahead])
    late = packed([far_y, from_behind, from_ahead], [total])
    late_core = other_core(late)
    rest_places = (
        (0, True), (0, False), (-2, True), (2, True), (-2, False), (2, False), (-3, True), (3, True), (4, True),
    )
    late_places = (
        (-3, False), (3, False), (4, False), (-1, True), (-1, False), (1, True), (1, False),
    )

    def on(places, same_core):
        return [(*place, same_core) for place in places]

    grads = gathered(
        me,
        own.shape[0],
        [
            (rest, on(rest_places, True)),
            (late, on(late_places, True)),
            (rest_core, on(rest_places, False)),
        ],
    )
    return grads, (late_core, on(late_places, False)), total


def weight_sums(place, total, pair):
    total = pair_sum(total, flip_z(total, 1), [pair])
    total = pair_sum(total, flip_z(total, 2))
    total = pair_sum(total, flip_z(total, 4))
    total = pair_sum(total, other_y(total))
    twin = other_core(total)
    first = place % 2 == 0
    return jnp.where(first, total, twin).astype(F32), jnp.where(first, twin, total).astype(F32)


def per_device(features, blocks, block_pos, counts, degree, w_self, w_neigh, cotangent):
    cycle_size = lax.axis_size("blk")
    group_size = lax.axis_size("grp")
    rows, width = features.shape
    place = lax.axis_index("grp").astype(jnp.int32)
    me = jnp.stack([place, lax.axis_index("blk").astype(jnp.int32)])
    even = place // 4 % 2 == 0
    table = (block_pos[0, 0], counts[0, 0], blocks[0, 0])

    feats = {(0, True): features, (0, False): flip_blk(features, 1)}
    for same in (True, False):
        for behind in (1, 3, 2):
            feats[behind, same] = along_blk(feats[0, same], 2 * behind)
    acc = slab_sums(me, [(0, True)], *table, [features])
    for sources in SLAB_STEPS[:-1]:
        acc = slab_sums(me, sources, *table, [feats[source] for source in sources], acc)
    sources = SLAB_STEPS[-1]
    shares = slab_parts(me, sources, *table, [feats[source] for source in sources], acc)
    parts = slab_reduced(me, rows, shares[:3], shares[3:])
    scale_deg = degree.astype(F32)[:, None]
    out, grad_slab, grad_self, mine, theirs = middle(
        me, features, cotangent, scale_deg, w_self, w_neigh, parts
    )

    grads, last, total = slab_gathered(me, even, grad_slab, mine, theirs)
    pairs = class_sums(me, *table, grads, last)
    arrived = [along_blk(pair, -2 * x) for pair, x in zip(pairs[:-1], CLASS_ORDER[:-1], strict=True)]
    arrived.append(pairs[-1])
    other = sums([[(pair, rows, rows) for pair in arrived]])[0]
    back_sum = wide_sum(grad_self, flip_blk(other, 1), *[pair[:rows] for pair in arrived])
    grad_x = back_sum.astype(BF16)

    total_self, total_neigh = weight_sums(place, total, pairs[0])
    norm_scale = 1.0 / math.sqrt(rows * cycle_size * group_size)
    return (out, grad_x, total_self * norm_scale, total_neigh * norm_scale)


def solution(mesh):
    in_specs = (
        P(("blk", "grp"), None),
        P("blk", "grp", None, None, None, None),
        P("blk", "grp", None, None),
        P("blk", "grp", None),
        P(("blk", "grp")),
        P(),
        P(),
        P(("blk", "grp"), None),
    )
    out_specs = (P(("blk", "grp"), None), P(("blk", "grp"), None), P(), P())
    return jax.shard_map(
        per_device, mesh=mesh, in_specs=in_specs, out_specs=out_specs, check_vma=False
    )
```

```python
import math

import jax
import jax.numpy as jnp
from jax import lax
from jax.experimental import pallas as pl
from jax.experimental.pallas import tpu as pltpu
from jax.sharding import PartitionSpec as P

BF16 = jnp.bfloat16
F32 = jnp.float32
GROUP = 12
MIB = 1 << 20
SMEM = pl.BlockSpec(memory_space=pltpu.SMEM)
VMEM = pl.BlockSpec(memory_space=pltpu.VMEM)
ANY = pl.BlockSpec(memory_space=pl.ANY)
KERNEL_VMEM = 24 * MIB
COST = pl.CostEstimate(flops=1024, bytes_accessed=1024, transcendentals=0)
SLAB_STEPS = (((1, True), (3, True), (2, True), (0, False)), ((1, False), (3, False), (2, False)))
CLASS_ORDER = (2, 1, 3, 0)

RING = 8


def along_grp(x, where):
    def target(i):
        z, y, c = where(i // 4, i // 2 % 2, i % 2)
        return z % RING * 4 + y * 2 + c

    return lax.ppermute(x, "grp", [(i, target(i)) for i in range(4 * RING)])


def other_core(x):
    return along_grp(x, lambda z, y, c: (z, y, 1 - c))


def other_y(x):
    return along_grp(x, lambda z, y, c: (z, 1 - y, c))


def along_z(x, distance):
    return along_grp(x, lambda z, y, c: (z + distance, y, c))


def two_along_z(x):
    return along_grp(x, lambda z, y, c: (z + 2 - z % 2 * 4, y, c))


def flip_z(x, bit):
    return along_grp(x, lambda z, y, c: (z ^ bit, y, c))


def along_blk(x, distance):
    n = lax.axis_size("blk")
    return lax.ppermute(x, "blk", [(i, (i + distance) % n) for i in range(n)])


def flip_blk(x, bit):
    n = lax.axis_size("blk")
    return lax.ppermute(x, "blk", [(i, i ^ bit) for i in range(n)])


def chunk_of(me, order, same_y, same_core):
    z, y, c = me // 4, me // 2 % 2, me % 2
    z = lax.rem(z + order + RING, RING)
    y = y if same_y else 1 - y
    c = c if same_core else 1 - c
    return z * 4 + y * 2 + c


def placed(block, col, live):
    zero = jnp.zeros_like(block)
    left = jnp.where(jnp.logical_and(live, col == 0), block, zero)
    right = jnp.where(jnp.logical_and(live, col == 1), block, zero)
    return left, right


def slab_lists(lists, pos_ref, counts_ref, blocks_ref, feats, acc):
    for k, feat_ref in zip(lists, feats, strict=True):
        live = counts_ref[k]
        feat = feat_ref[...]

        def step(s, _, k=k, live=live, feat=feat):
            rows, places = [], []
            for u in range(GROUP):
                j = s * GROUP + u
                p = pos_ref[k, j]
                left, right = placed(blocks_ref[k, j], p % 2, j < live)
                rows.append(jnp.concatenate([left, right], axis=1))
                places.append(p // 2)
            products = jnp.dot(jnp.concatenate(rows, axis=0), feat, preferred_element_type=F32)
            tile = rows[0].shape[0]
            for u in range(GROUP):
                acc[places[u]] += products[u * tile : (u + 1) * tile]
            return 0

        lax.fori_loop(0, (live + GROUP - 1) // GROUP, step, 0)


def list_of(blk, source):
    behind, same = source
    y = blk % 2
    return (2 * behind + (0 if same else 2 * y - 1) + 8) % 8


def slab_sums(me, sources, block_pos, counts, blocks, feats, acc=None):
    _, slots, tile, _ = blocks.shape
    rows, width = feats[0].shape
    shape = jax.ShapeDtypeStruct((4 * RING * rows // tile, tile, width), F32)

    def kernel(me_ref, pos_ref, counts_ref, blocks_ref, *refs):
        out = refs[-1]
        lists = [list_of(me_ref[1], source) for source in sources]
        if acc is None:

            def clear(i, _):
                out[i] = jnp.zeros(out.shape[1:], F32)
                return 0

            lax.fori_loop(0, out.shape[0], clear, 0)
        slab_lists(lists, pos_ref, counts_ref, blocks_ref, refs[: len(sources)], out)

    more = [] if acc is None else [acc]
    return pl.pallas_call(
        kernel,
        out_shape=shape,
        in_specs=[SMEM, SMEM, SMEM, VMEM] + [VMEM] * (len(feats) + len(more)),
        out_specs=VMEM,
        input_output_aliases={4 + len(feats): 0} if more else {},
        compiler_params=pltpu.CompilerParams(vmem_limit_bytes=KERNEL_VMEM),
        cost_estimate=COST,
        name="slab_sums",
    )(me, block_pos, counts, blocks, *feats, *more)


FAR_Y = ((3, False), (-3, False), (4, False))
NEAR = ((1, True), (1, False), (-1, True), (-1, False), (2, False), (-2, False))
REST = ((3, True), (-3, True), (4, True), (2, True), (-2, True), (0, False), (0, True))


def slab_parts(me, sources, block_pos, counts, blocks, feats, acc):
    _, slots, tile, _ = blocks.shape
    rows, width = feats[0].shape
    groups = (FAR_Y, NEAR, REST)

    def kernel(me_ref, pos_ref, counts_ref, blocks_ref, *refs):
        total, outs = refs[len(sources)], refs[len(sources) + 1 :]
        lists = [list_of(me_ref[1], source) for source in sources]
        slab_lists(lists, pos_ref, counts_ref, blocks_ref, refs[: len(sources)], total)
        mine = me_ref[0]
        for out, (same_core, group) in zip(
            outs, [(same, group) for same in (False, True) for group in groups], strict=True
        ):
            for i, (order, same_y) in enumerate(group):
                chunk = chunk_of(mine, order, same_y, same_core)
                for half in range(2):
                    start = (2 * i + half) * tile
                    out[start : start + tile, :] = total[chunk * 2 + half].astype(BF16)

    return pl.pallas_call(
        kernel,
        out_shape=[
            jax.ShapeDtypeStruct((len(group) * rows, width), BF16) for group in groups * 2
        ],
        in_specs=[SMEM, SMEM, SMEM, VMEM] + [VMEM] * (len(feats) + 1),
        out_specs=[VMEM] * 6,
        compiler_params=pltpu.CompilerParams(vmem_limit_bytes=KERNEL_VMEM),
        cost_estimate=COST,
        name="slab_parts",
    )(me, block_pos, counts, blocks, *feats, acc)


def mid_kernel(refs_in, refs_out):
    me_ref, feats, cotangent, degree, w_self, w_neigh, parts = refs_in
    out, grad_slab, grad_self, mine, theirs = refs_out
    deg = degree[...]
    summed = parts[0][...].astype(F32)
    for part in parts[1:]:
        summed = summed + part[...].astype(F32)
    mean = (summed / deg).astype(BF16)
    x, ws, wn = feats[...], w_self[...], w_neigh[...]
    pre = jnp.dot(x, ws, preferred_element_type=F32) + jnp.dot(mean, wn, preferred_element_type=F32)
    sigma = jax.nn.sigmoid(pre)
    out[...] = (pre * sigma).astype(BF16)
    grad = (cotangent[...].astype(F32) * sigma * (1.0 + pre * (1.0 - sigma))).astype(BF16)
    transposed = (((1,), (1,)), ((), ()))
    back = lax.dot_general(grad, wn, transposed, preferred_element_type=F32)
    grad_slab[...] = (back / deg).astype(BF16)
    grad_self[...] = lax.dot_general(grad, ws, transposed, preferred_element_type=F32)
    over_rows = (((0,), (0,)), ((), ()))
    local_self = lax.dot_general(x, grad, over_rows, preferred_element_type=F32).astype(BF16)
    local_neigh = lax.dot_general(mean, grad, over_rows, preferred_element_type=F32).astype(BF16)
    first = me_ref[0] % 2 == 0
    mine[...] = jnp.where(first, local_self, local_neigh)
    theirs[...] = jnp.where(first, local_neigh, local_self)


def middle(me, feats, cotangent, degree, w_self, w_neigh, parts):
    rows, width = feats.shape

    def kernel(*refs):
        mid_kernel((*refs[:6], refs[6 : 6 + len(parts)]), refs[6 + len(parts) :])

    low, wide = jax.ShapeDtypeStruct((rows, width), BF16), jax.ShapeDtypeStruct((rows, width), F32)
    square = jax.ShapeDtypeStruct((width, width), BF16)
    return pl.pallas_call(
        kernel,
        out_shape=(low, low, wide, square, square),
        in_specs=[SMEM] + [VMEM] * (5 + len(parts)),
        out_specs=(VMEM,) * 5,
        compiler_params=pltpu.CompilerParams(vmem_limit_bytes=16 * MIB),
        cost_estimate=COST,
        name="middle",
    )(me, feats, cotangent, degree, w_self, w_neigh, *parts)


def put(grads, chunk, value):
    tile = grads.shape[1]
    for half in range(2):
        grads[chunk * 2 + half] = value[half * tile : (half + 1) * tile]


def gathered(me, rows, pieces, after=()):
    width, tile = pieces[0][0].shape[1], rows // 2

    def kernel(me_ref, *refs):
        mine, out = me_ref[0], refs[-1]
        for ref, (_, places) in zip(refs[: len(pieces)], pieces, strict=True):
            for i, place in enumerate(places):
                put(out, chunk_of(mine, *place), ref[i * rows : (i + 1) * rows, :])

    return pl.pallas_call(
        kernel,
        out_shape=jax.ShapeDtypeStruct((4 * RING * 2, tile, width), BF16),
        in_specs=[SMEM] + [VMEM] * len(pieces) + [ANY] * len(after),
        out_specs=VMEM,
        compiler_params=pltpu.CompilerParams(vmem_limit_bytes=KERNEL_VMEM),
        cost_estimate=COST,
        name="gathered",
    )(me, *[array for array, _ in pieces], *after)


def packed(arrays, after=()):
    starts = [0]
    for array in arrays:
        starts.append(starts[-1] + array.shape[0])

    def kernel(*refs):
        for ref, start, end in zip(refs[: len(arrays)], starts[:-1], starts[1:], strict=True):
            refs[-1][start:end, :] = ref[...]

    return pl.pallas_call(
        kernel,
        out_shape=jax.ShapeDtypeStruct((starts[-1], arrays[0].shape[1]), BF16),
        in_specs=[VMEM] * len(arrays) + [ANY] * len(after),
        out_specs=VMEM,
        compiler_params=pltpu.CompilerParams(vmem_limit_bytes=KERNEL_VMEM),
        cost_estimate=COST,
        name="packed",
    )(*arrays, *after)


def class_list(k, pos_ref, counts_ref, blocks_ref, grads, out):
    live = counts_ref[k]

    def step(s, total):
        cols, picked = [], []
        for u in range(GROUP):
            j = s * GROUP + u
            p = pos_ref[k, j]
            top, bottom = placed(blocks_ref[k, j].T, p % 2, j < live)
            cols.append(jnp.concatenate([top, bottom], axis=0))
            picked.append(grads[p // 2])
        return total + jnp.dot(
            jnp.concatenate(cols, axis=1),
            jnp.concatenate(picked, axis=0),
            preferred_element_type=F32,
        )

    out[...] = lax.fori_loop(
        0, (live + GROUP - 1) // GROUP, step, jnp.zeros(out.shape, F32)
    ).astype(out.dtype)


def class_sums(me, block_pos, counts, blocks, grads, last):
    _, slots, tile, _ = blocks.shape
    width = grads.shape[2]
    rows = 2 * tile

    def kernel(me_ref, pos_ref, counts_ref, blocks_ref, _, last_ref, grads_ref, *outs):
        for i, place in enumerate(last[1]):
            put(grads_ref, chunk_of(me_ref[0], *place), last_ref[i * rows : (i + 1) * rows, :])
        for behind, out in zip(CLASS_ORDER, outs, strict=True):
            for i, same in enumerate((True, False)):
                k = list_of(me_ref[1], (behind, same))
                view = out.at[pl.ds(i * rows, rows), :]
                class_list(k, pos_ref, counts_ref, blocks_ref, grads_ref, view)

    pair = jax.ShapeDtypeStruct((2 * rows, width), BF16)
    return pl.pallas_call(
        kernel,
        out_shape=[jax.ShapeDtypeStruct(grads.shape, BF16)] + [pair] * len(CLASS_ORDER),
        in_specs=[SMEM, SMEM, SMEM] + [VMEM] * 3,
        out_specs=[VMEM] * (1 + len(CLASS_ORDER)),
        input_output_aliases={4: 0},
        compiler_params=pltpu.CompilerParams(vmem_limit_bytes=KERNEL_VMEM),
        cost_estimate=COST,
        name="class_sums",
    )(me, block_pos, counts, blocks, grads, last[0])[1:]


def wide_sum(*terms):
    total = terms[0].astype(F32)
    for term in terms[1:]:
        total = total + term.astype(F32)
    return total


def sums(outs, after=(), me=None):
    arrays = []
    for terms in outs:
        for array, *_ in terms:
            if not any(array is other for other in arrays):
                arrays.append(array)

    def find(array):
        return next(i for i, other in enumerate(arrays) if other is array)

    scalars = [] if me is None else [me]

    def kernel(*refs):
        me_refs, refs = refs[: len(scalars)], refs[len(scalars) :]
        for out, terms in zip(refs[len(arrays) + len(after) :], outs, strict=True):
            total = None
            for array, first, count, *parity in terms:
                term = refs[find(array)][first : first + count, :].astype(F32)
                if parity:
                    mine = me_refs[0][0] // 4 % 2 == parity[0]
                    term = jnp.where(mine, term, jnp.zeros_like(term))
                total = term if total is None else total + term
            out[...] = total.astype(BF16)

    width = arrays[0].shape[1]
    return pl.pallas_call(
        kernel,
        out_shape=[jax.ShapeDtypeStruct((terms[0][2], width), BF16) for terms in outs],
        in_specs=[SMEM] * len(scalars) + [VMEM] * len(arrays) + [ANY] * len(after),
        out_specs=[VMEM] * len(outs),
        compiler_params=pltpu.CompilerParams(vmem_limit_bytes=KERNEL_VMEM),
        cost_estimate=COST,
        name="sums",
    )(*scalars, *arrays, *after)


def pair_sum(first, second, after=()):
    rows = first.shape[0]
    return sums([[(first, 0, rows), (second, 0, rows)]], after)[0]


def slab_reduced(me, rows, sent, kept):
    def at(array, first, count=1):
        return array[first * rows : (first + count) * rows]

    def both(first, count, *arrays):
        return [(array, first * rows, count * rows) for array in arrays]

    far_y = other_y(pair_sum(kept[0], other_core(sent[0])))
    near, more = kept[1], other_core(sent[1])
    ahead, behind, mid = sums([both(first, 2, near, more) for first in (0, 2, 4)])
    from_behind, from_ahead = along_z(ahead, 1), along_z(behind, -1)
    mid_y = other_y(mid)
    rest, more = kept[2], other_core(sent[2])
    ahead, behind, opposite = sums(
        [both(i, 1, rest, more, far_y) for i in range(3)], [from_behind, from_ahead]
    )
    three_ahead, three_behind = along_z(ahead, 1), along_z(behind, -1)
    opposite = two_along_z(opposite)
    one = (0, rows)
    two_ahead, two_behind = sums(
        [
            [*both(3, 1, rest, more), *both(0, 1, mid_y), (three_ahead, *one), (opposite, *one, 0)],
            [*both(4, 1, rest, more), *both(1, 1, mid_y), (three_behind, *one), (opposite, *one, 1)],
        ],
        me=me,
    )
    from_two_behind, from_two_ahead = along_z(two_ahead, 2), along_z(two_behind, -2)
    own_y = other_y(
        sums([both(5, 1, rest, more) + both(1, 1, from_behind, from_ahead)], [three_ahead])[0]
    )
    base = wide_sum(at(rest, 6), at(more, 6), at(from_behind, 0), at(from_ahead, 0))
    return [base, own_y, from_two_behind, from_two_ahead]


def slab_gathered(me, even, own, mine, theirs):
    behind2, ahead2 = along_z(own, 2), along_z(own, -2)
    own_y = other_y(own)
    behind3, ahead3 = along_z(behind2, 1), along_z(ahead2, -1)
    opposite = two_along_z(jnp.where(even, behind2, ahead2))
    total = pair_sum(mine, other_core(packed([theirs], [own_y])), [behind2, ahead2])
    mid_y = other_y(packed([behind2, ahead2], [total]))
    total = pair_sum(total, flip_blk(total, 2), [behind3, ahead3])
    far = packed([behind3, ahead3, opposite], [mid_y, total])
    far_y = other_y(far)
    total = pair_sum(total, flip_blk(total, 4), [far])
    both = packed([own, own_y], [total])
    from_behind, from_ahead = along_z(both, 1), along_z(both, -1)
    rest = packed([own, own_y, behind2, ahead2, mid_y, far])
    rest_core = other_core(rest)
    total = pair_sum(total, flip_blk(total, 1), [from_behind, from_ahead])
    late = packed([far_y, from_behind, from_ahead], [total])
    late_core = other_core(late)
    rest_places = (
        (0, True), (0, False), (-2, True), (2, True), (-2, False), (2, False), (-3, True), (3, True), (4, True),
    )
    late_places = (
        (-3, False), (3, False), (4, False), (-1, True), (-1, False), (1, True), (1, False),
    )

    def on(places, same_core):
        return [(*place, same_core) for place in places]

    grads = gathered(
        me,
        own.shape[0],
        [
            (rest, on(rest_places, True)),
            (late, on(late_places, True)),
            (rest_core, on(rest_places, False)),
        ],
    )
    return grads, (late_core, on(late_places, False)), total


def weight_sums(place, total, pair):
    total = pair_sum(total, flip_z(total, 4), [pair])
    total = pair_sum(total, flip_z(total, 2))
    total = pair_sum(total, flip_z(total, 1))
    total = pair_sum(total, other_y(total))
    twin = other_core(total)
    first = place % 2 == 0
    return jnp.where(first, total, twin).astype(F32), jnp.where(first, twin, total).astype(F32)


def per_device(features, blocks, block_pos, counts, degree, w_self, w_neigh, cotangent):
    cycle_size = lax.axis_size("blk")
    group_size = lax.axis_size("grp")
    rows, width = features.shape
    place = lax.axis_index("grp").astype(jnp.int32)
    me = jnp.stack([place, lax.axis_index("blk").astype(jnp.int32)])
    even = place // 4 % 2 == 0
    table = (block_pos[0, 0], counts[0, 0], blocks[0, 0])

    feats = {(0, True): features, (0, False): flip_blk(features, 1)}
    for same in (True, False):
        for behind in (1, 3, 2):
            feats[behind, same] = along_blk(feats[0, same], 2 * behind)
    acc = slab_sums(me, [(0, True)], *table, [features])
    for sources in SLAB_STEPS[:-1]:
        acc = slab_sums(me, sources, *table, [feats[source] for source in sources], acc)
    sources = SLAB_STEPS[-1]
    shares = slab_parts(me, sources, *table, [feats[source] for source in sources], acc)
    parts = slab_reduced(me, rows, shares[:3], shares[3:])
    scale_deg = degree.astype(F32)[:, None]
    out, grad_slab, grad_self, mine, theirs = middle(
        me, features, cotangent, scale_deg, w_self, w_neigh, parts
    )

    grads, last, total = slab_gathered(me, even, grad_slab, mine, theirs)
    pairs = class_sums(me, *table, grads, last)
    arrived = [along_blk(pair, -2 * x) for pair, x in zip(pairs[:-1], CLASS_ORDER[:-1], strict=True)]
    arrived.append(pairs[-1])
    other = sums([[(pair, rows, rows) for pair in arrived]])[0]
    back_sum = wide_sum(grad_self, flip_blk(other, 1), *[pair[:rows] for pair in arrived])
    grad_x = back_sum.astype(BF16)

    total_self, total_neigh = weight_sums(place, total, pairs[0])
    norm_scale = 1.0 / math.sqrt(rows * cycle_size * group_size)
    return (out, grad_x, total_self * norm_scale, total_neigh * norm_scale)


def solution(mesh):
    in_specs = (
        P(("blk", "grp"), None),
        P("blk", "grp", None, None, None, None),
        P("blk", "grp", None, None),
        P("blk", "grp", None),
        P(("blk", "grp")),
        P(),
        P(),
        P(("blk", "grp"), None),
    )
    out_specs = (P(("blk", "grp"), None), P(("blk", "grp"), None), P(), P())
    return jax.shard_map(
        per_device, mesh=mesh, in_specs=in_specs, out_specs=out_specs, check_vma=False
    )
```

```python
import math

import jax
import jax.numpy as jnp
from jax import lax
from jax.experimental import pallas as pl
from jax.experimental.pallas import tpu as pltpu
from jax.sharding import PartitionSpec as P

BF16 = jnp.bfloat16
F32 = jnp.float32
GROUP = 12
MIB = 1 << 20
SMEM = pl.BlockSpec(memory_space=pltpu.SMEM)
VMEM = pl.BlockSpec(memory_space=pltpu.VMEM)
ANY = pl.BlockSpec(memory_space=pl.ANY)
KERNEL_VMEM = 24 * MIB
COST = pl.CostEstimate(flops=1024, bytes_accessed=1024, transcendentals=0)
SLAB_STEPS = (((1, True), (3, True), (2, True), (0, False)), ((1, False), (3, False), (2, False)))
CLASS_ORDER = (2, 1, 3, 0)

RING = 8


def along_grp(x, where):
    def target(i):
        z, y, c = where(i // 4, i // 2 % 2, i % 2)
        return z % RING * 4 + y * 2 + c

    return lax.ppermute(x, "grp", [(i, target(i)) for i in range(4 * RING)])


def other_core(x):
    return along_grp(x, lambda z, y, c: (z, y, 1 - c))


def other_y(x):
    return along_grp(x, lambda z, y, c: (z, 1 - y, c))


def along_z(x, distance):
    return along_grp(x, lambda z, y, c: (z + distance, y, c))


def two_along_z(x):
    return along_grp(x, lambda z, y, c: (z + 2 - z % 2 * 4, y, c))


def flip_z(x, bit):
    return along_grp(x, lambda z, y, c: (z ^ bit, y, c))


def along_blk(x, distance):
    n = lax.axis_size("blk")
    return lax.ppermute(x, "blk", [(i, (i + distance) % n) for i in range(n)])


def flip_blk(x, bit):
    n = lax.axis_size("blk")
    return lax.ppermute(x, "blk", [(i, i ^ bit) for i in range(n)])


def chunk_of(me, order, same_y, same_core):
    z, y, c = me // 4, me // 2 % 2, me % 2
    z = lax.rem(z + order + RING, RING)
    y = y if same_y else 1 - y
    c = c if same_core else 1 - c
    return z * 4 + y * 2 + c


def placed(block, col, live):
    zero = jnp.zeros_like(block)
    left = jnp.where(jnp.logical_and(live, col == 0), block, zero)
    right = jnp.where(jnp.logical_and(live, col == 1), block, zero)
    return left, right


def slab_lists(lists, pos_ref, counts_ref, blocks_ref, feats, acc):
    for k, feat_ref in zip(lists, feats, strict=True):
        live = counts_ref[k]
        feat = feat_ref[...]

        def step(s, _, k=k, live=live, feat=feat):
            rows, places = [], []
            for u in range(GROUP):
                j = s * GROUP + u
                p = pos_ref[k, j]
                left, right = placed(blocks_ref[k, j], p % 2, j < live)
                rows.append(jnp.concatenate([left, right], axis=1))
                places.append(p // 2)
            products = jnp.dot(jnp.concatenate(rows, axis=0), feat, preferred_element_type=F32)
            tile = rows[0].shape[0]
            for u in range(GROUP):
                acc[places[u]] += products[u * tile : (u + 1) * tile]
            return 0

        lax.fori_loop(0, (live + GROUP - 1) // GROUP, step, 0)


def list_of(blk, source):
    behind, same = source
    y = blk % 2
    return (2 * behind + (0 if same else 2 * y - 1) + 8) % 8


def slab_sums(me, sources, block_pos, counts, blocks, feats, acc=None):
    _, slots, tile, _ = blocks.shape
    rows, width = feats[0].shape
    shape = jax.ShapeDtypeStruct((4 * RING * rows // tile, tile, width), F32)

    def kernel(me_ref, pos_ref, counts_ref, blocks_ref, *refs):
        out = refs[-1]
        lists = [list_of(me_ref[1], source) for source in sources]
        if acc is None:

            def clear(i, _):
                out[i] = jnp.zeros(out.shape[1:], F32)
                return 0

            lax.fori_loop(0, out.shape[0], clear, 0)
        slab_lists(lists, pos_ref, counts_ref, blocks_ref, refs[: len(sources)], out)

    more = [] if acc is None else [acc]
    return pl.pallas_call(
        kernel,
        out_shape=shape,
        in_specs=[SMEM, SMEM, SMEM, VMEM] + [VMEM] * (len(feats) + len(more)),
        out_specs=VMEM,
        input_output_aliases={4 + len(feats): 0} if more else {},
        compiler_params=pltpu.CompilerParams(vmem_limit_bytes=KERNEL_VMEM),
        cost_estimate=COST,
        name="slab_sums",
    )(me, block_pos, counts, blocks, *feats, *more)


FAR_Y = ((3, False), (-3, False), (4, False))
NEAR = ((1, True), (1, False), (-1, True), (-1, False), (2, False), (-2, False))
REST = ((3, True), (-3, True), (4, True), (2, True), (-2, True), (0, False), (0, True))


def slab_parts(me, sources, block_pos, counts, blocks, feats, acc):
    _, slots, tile, _ = blocks.shape
    rows, width = feats[0].shape
    groups = (FAR_Y, NEAR, REST)

    def kernel(me_ref, pos_ref, counts_ref, blocks_ref, *refs):
        total, outs = refs[len(sources)], refs[len(sources) + 1 :]
        lists = [list_of(me_ref[1], source) for source in sources]
        slab_lists(lists, pos_ref, counts_ref, blocks_ref, refs[: len(sources)], total)
        mine = me_ref[0]
        for out, (same_core, group) in zip(
            outs, [(same, group) for same in (False, True) for group in groups], strict=True
        ):
            for i, (order, same_y) in enumerate(group):
                chunk = chunk_of(mine, order, same_y, same_core)
                for half in range(2):
                    start = (2 * i + half) * tile
                    out[start : start + tile, :] = total[chunk * 2 + half].astype(BF16)

    return pl.pallas_call(
        kernel,
        out_shape=[
            jax.ShapeDtypeStruct((len(group) * rows, width), BF16) for group in groups * 2
        ],
        in_specs=[SMEM, SMEM, SMEM, VMEM] + [VMEM] * (len(feats) + 1),
        out_specs=[VMEM] * 6,
        compiler_params=pltpu.CompilerParams(vmem_limit_bytes=KERNEL_VMEM),
        cost_estimate=COST,
        name="slab_parts",
    )(me, block_pos, counts, blocks, *feats, acc)


def mid_kernel(refs_in, refs_out):
    me_ref, feats, cotangent, degree, w_self, w_neigh, parts = refs_in
    out, grad_slab, grad_self, mine, theirs = refs_out
    deg = degree[...]
    summed = parts[0][...].astype(F32)
    for part in parts[1:]:
        summed = summed + part[...].astype(F32)
    mean = (summed / deg).astype(BF16)
    x, ws, wn = feats[...], w_self[...], w_neigh[...]
    pre = jnp.dot(x, ws, preferred_element_type=F32) + jnp.dot(mean, wn, preferred_element_type=F32)
    sigma = jax.nn.sigmoid(pre)
    out[...] = (pre * sigma).astype(BF16)
    grad = (cotangent[...].astype(F32) * sigma * (1.0 + pre * (1.0 - sigma))).astype(BF16)
    transposed = (((1,), (1,)), ((), ()))
    back = lax.dot_general(grad, wn, transposed, preferred_element_type=F32)
    grad_slab[...] = (back / deg).astype(BF16)
    grad_self[...] = lax.dot_general(grad, ws, transposed, preferred_element_type=F32)
    over_rows = (((0,), (0,)), ((), ()))
    local_self = lax.dot_general(x, grad, over_rows, preferred_element_type=F32).astype(BF16)
    local_neigh = lax.dot_general(mean, grad, over_rows, preferred_element_type=F32).astype(BF16)
    first = me_ref[0] % 2 == 0
    mine[...] = jnp.where(first, local_self, local_neigh)
    theirs[...] = jnp.where(first, local_neigh, local_self)


def middle(me, feats, cotangent, degree, w_self, w_neigh, parts):
    rows, width = feats.shape

    def kernel(*refs):
        mid_kernel((*refs[:6], refs[6 : 6 + len(parts)]), refs[6 + len(parts) :])

    low, wide = jax.ShapeDtypeStruct((rows, width), BF16), jax.ShapeDtypeStruct((rows, width), F32)
    square = jax.ShapeDtypeStruct((width, width), BF16)
    return pl.pallas_call(
        kernel,
        out_shape=(low, low, wide, square, square),
        in_specs=[SMEM] + [VMEM] * (5 + len(parts)),
        out_specs=(VMEM,) * 5,
        compiler_params=pltpu.CompilerParams(vmem_limit_bytes=16 * MIB),
        cost_estimate=COST,
        name="middle",
    )(me, feats, cotangent, degree, w_self, w_neigh, *parts)


def put(grads, chunk, value):
    tile = grads.shape[1]
    for half in range(2):
        grads[chunk * 2 + half] = value[half * tile : (half + 1) * tile]


def gathered(me, rows, pieces, after=()):
    width, tile = pieces[0][0].shape[1], rows // 2

    def kernel(me_ref, *refs):
        mine, out = me_ref[0], refs[-1]
        for ref, (_, places) in zip(refs[: len(pieces)], pieces, strict=True):
            for i, place in enumerate(places):
                put(out, chunk_of(mine, *place), ref[i * rows : (i + 1) * rows, :])

    return pl.pallas_call(
        kernel,
        out_shape=jax.ShapeDtypeStruct((4 * RING * 2, tile, width), BF16),
        in_specs=[SMEM] + [VMEM] * len(pieces) + [ANY] * len(after),
        out_specs=VMEM,
        compiler_params=pltpu.CompilerParams(vmem_limit_bytes=KERNEL_VMEM),
        cost_estimate=COST,
        name="gathered",
    )(me, *[array for array, _ in pieces], *after)


def packed(arrays, after=()):
    starts = [0]
    for array in arrays:
        starts.append(starts[-1] + array.shape[0])

    def kernel(*refs):
        for ref, start, end in zip(refs[: len(arrays)], starts[:-1], starts[1:], strict=True):
            refs[-1][start:end, :] = ref[...]

    return pl.pallas_call(
        kernel,
        out_shape=jax.ShapeDtypeStruct((starts[-1], arrays[0].shape[1]), BF16),
        in_specs=[VMEM] * len(arrays) + [ANY] * len(after),
        out_specs=VMEM,
        compiler_params=pltpu.CompilerParams(vmem_limit_bytes=KERNEL_VMEM),
        cost_estimate=COST,
        name="packed",
    )(*arrays, *after)


def class_list(k, pos_ref, counts_ref, blocks_ref, grads, out):
    live = counts_ref[k]

    def step(s, total):
        cols, picked = [], []
        for u in range(GROUP):
            j = s * GROUP + u
            p = pos_ref[k, j]
            top, bottom = placed(blocks_ref[k, j].T, p % 2, j < live)
            cols.append(jnp.concatenate([top, bottom], axis=0))
            picked.append(grads[p // 2])
        return total + jnp.dot(
            jnp.concatenate(cols, axis=1),
            jnp.concatenate(picked, axis=0),
            preferred_element_type=F32,
        )

    out[...] = lax.fori_loop(
        0, (live + GROUP - 1) // GROUP, step, jnp.zeros(out.shape, F32)
    ).astype(out.dtype)


def class_sums(me, block_pos, counts, blocks, grads, last):
    _, slots, tile, _ = blocks.shape
    width = grads.shape[2]
    rows = 2 * tile

    def kernel(me_ref, pos_ref, counts_ref, blocks_ref, _, last_ref, grads_ref, *outs):
        for i, place in enumerate(last[1]):
            put(grads_ref, chunk_of(me_ref[0], *place), last_ref[i * rows : (i + 1) * rows, :])
        for behind, out in zip(CLASS_ORDER, outs, strict=True):
            for i, same in enumerate((True, False)):
                k = list_of(me_ref[1], (behind, same))
                view = out.at[pl.ds(i * rows, rows), :]
                class_list(k, pos_ref, counts_ref, blocks_ref, grads_ref, view)

    pair = jax.ShapeDtypeStruct((2 * rows, width), BF16)
    return pl.pallas_call(
        kernel,
        out_shape=[jax.ShapeDtypeStruct(grads.shape, BF16)] + [pair] * len(CLASS_ORDER),
        in_specs=[SMEM, SMEM, SMEM] + [VMEM] * 3,
        out_specs=[VMEM] * (1 + len(CLASS_ORDER)),
        input_output_aliases={4: 0},
        compiler_params=pltpu.CompilerParams(vmem_limit_bytes=KERNEL_VMEM),
        cost_estimate=COST,
        name="class_sums",
    )(me, block_pos, counts, blocks, grads, last[0])[1:]


def wide_sum(*terms):
    total = terms[0].astype(F32)
    for term in terms[1:]:
        total = total + term.astype(F32)
    return total


def sums(outs, after=(), me=None):
    arrays = []
    for terms in outs:
        for array, *_ in terms:
            if not any(array is other for other in arrays):
                arrays.append(array)

    def find(array):
        return next(i for i, other in enumerate(arrays) if other is array)

    scalars = [] if me is None else [me]

    def kernel(*refs):
        me_refs, refs = refs[: len(scalars)], refs[len(scalars) :]
        for out, terms in zip(refs[len(arrays) + len(after) :], outs, strict=True):
            total = None
            for array, first, count, *parity in terms:
                term = refs[find(array)][first : first + count, :].astype(F32)
                if parity:
                    mine = me_refs[0][0] // 4 % 2 == parity[0]
                    term = jnp.where(mine, term, jnp.zeros_like(term))
                total = term if total is None else total + term
            out[...] = total.astype(BF16)

    width = arrays[0].shape[1]
    return pl.pallas_call(
        kernel,
        out_shape=[jax.ShapeDtypeStruct((terms[0][2], width), BF16) for terms in outs],
        in_specs=[SMEM] * len(scalars) + [VMEM] * len(arrays) + [ANY] * len(after),
        out_specs=[VMEM] * len(outs),
        compiler_params=pltpu.CompilerParams(vmem_limit_bytes=KERNEL_VMEM),
        cost_estimate=COST,
        name="sums",
    )(*scalars, *arrays, *after)


def pair_sum(first, second, after=()):
    rows = first.shape[0]
    return sums([[(first, 0, rows), (second, 0, rows)]], after)[0]


def slab_reduced(me, rows, sent, kept):
    def at(array, first, count=1):
        return array[first * rows : (first + count) * rows]

    def both(first, count, *arrays):
        return [(array, first * rows, count * rows) for array in arrays]

    far_y = other_y(pair_sum(kept[0], other_core(sent[0])))
    near, more = kept[1], other_core(sent[1])
    ahead, behind, mid = sums([both(first, 2, near, more) for first in (0, 2, 4)])
    from_behind, from_ahead = along_z(ahead, 1), along_z(behind, -1)
    mid_y = other_y(mid)
    rest, more = kept[2], other_core(sent[2])
    ahead, behind, opposite = sums(
        [both(i, 1, rest, more, far_y) for i in range(3)], [from_behind, from_ahead]
    )
    three_ahead, three_behind = along_z(ahead, 1), along_z(behind, -1)
    opposite = two_along_z(opposite)
    one = (0, rows)
    two_ahead, two_behind = sums(
        [
            [*both(3, 1, rest, more), *both(0, 1, mid_y), (three_ahead, *one), (opposite, *one, 0)],
            [*both(4, 1, rest, more), *both(1, 1, mid_y), (three_behind, *one), (opposite, *one, 1)],
        ],
        me=me,
    )
    from_two_behind, from_two_ahead = along_z(two_ahead, 2), along_z(two_behind, -2)
    own_y = other_y(
        sums([both(5, 1, rest, more) + both(1, 1, from_behind, from_ahead)], [three_ahead])[0]
    )
    base = wide_sum(at(rest, 6), at(more, 6), at(from_behind, 0), at(from_ahead, 0))
    return [base, own_y, from_two_behind, from_two_ahead]


def slab_gathered(me, even, own, mine, theirs):
    behind2, ahead2 = along_z(own, 2), along_z(own, -2)
    own_y = other_y(own)
    behind3, ahead3 = along_z(behind2, 1), along_z(ahead2, -1)
    opposite = two_along_z(jnp.where(even, behind2, ahead2))
    total = pair_sum(mine, other_core(packed([theirs], [own_y])), [behind2, ahead2])
    mid_y = other_y(packed([behind2, ahead2], [total]))
    total = pair_sum(total, flip_blk(total, 2), [behind3, ahead3])
    far = packed([behind3, ahead3, opposite], [mid_y, total])
    far_y = other_y(far)
    total = pair_sum(total, flip_blk(total, 4), [far])
    both = packed([own, own_y], [total])
    from_behind, from_ahead = along_z(both, 1), along_z(both, -1)
    total = pair_sum(total, flip_blk(total, 1), [from_behind, from_ahead])
    half = packed(
        [own, own_y, behind2, ahead2, mid_y, far, far_y, from_behind, from_ahead], [total]
    )
    half_core = other_core(half)
    places = (
        (0, True), (0, False), (-2, True), (2, True), (-2, False), (2, False), (-3, True), (3, True), (4, True),
        (-3, False), (3, False), (4, False), (-1, True), (-1, False), (1, True), (1, False),
    )

    def on(places, same_core):
        return [(*place, same_core) for place in places]

    grads = gathered(me, own.shape[0], [(half, on(places, True))])
    return grads, (half_core, on(places, False)), total


def weight_sums(place, total, pair):
    total = pair_sum(total, flip_z(total, 4), [pair])
    total = pair_sum(total, flip_z(total, 2))
    total = pair_sum(total, flip_z(total, 1))
    total = pair_sum(total, other_y(total))
    twin = other_core(total)
    first = place % 2 == 0
    return jnp.where(first, total, twin).astype(F32), jnp.where(first, twin, total).astype(F32)


def per_device(features, blocks, block_pos, counts, degree, w_self, w_neigh, cotangent):
    cycle_size = lax.axis_size("blk")
    group_size = lax.axis_size("grp")
    rows, width = features.shape
    place = lax.axis_index("grp").astype(jnp.int32)
    me = jnp.stack([place, lax.axis_index("blk").astype(jnp.int32)])
    even = place // 4 % 2 == 0
    table = (block_pos[0, 0], counts[0, 0], blocks[0, 0])

    feats = {(0, True): features, (0, False): flip_blk(features, 1)}
    for same in (True, False):
        for behind in (1, 3, 2):
            feats[behind, same] = along_blk(feats[0, same], 2 * behind)
    acc = slab_sums(me, [(0, True)], *table, [features])
    for sources in SLAB_STEPS[:-1]:
        acc = slab_sums(me, sources, *table, [feats[source] for source in sources], acc)
    sources = SLAB_STEPS[-1]
    shares = slab_parts(me, sources, *table, [feats[source] for source in sources], acc)
    parts = slab_reduced(me, rows, shares[:3], shares[3:])
    scale_deg = degree.astype(F32)[:, None]
    out, grad_slab, grad_self, mine, theirs = middle(
        me, features, cotangent, scale_deg, w_self, w_neigh, parts
    )

    grads, last, total = slab_gathered(me, even, grad_slab, mine, theirs)
    pairs = class_sums(me, *table, grads, last)
    arrived = [along_blk(pair, -2 * x) for pair, x in zip(pairs[:-1], CLASS_ORDER[:-1], strict=True)]
    arrived.append(pairs[-1])
    other = sums([[(pair, rows, rows) for pair in arrived]])[0]
    back_sum = wide_sum(grad_self, flip_blk(other, 1), *[pair[:rows] for pair in arrived])
    grad_x = back_sum.astype(BF16)

    total_self, total_neigh = weight_sums(place, total, pairs[0])
    norm_scale = 1.0 / math.sqrt(rows * cycle_size * group_size)
    return (out, grad_x, total_self * norm_scale, total_neigh * norm_scale)


def solution(mesh):
    in_specs = (
        P(("blk", "grp"), None),
        P("blk", "grp", None, None, None, None),
        P("blk", "grp", None, None),
        P("blk", "grp", None),
        P(("blk", "grp")),
        P(),
        P(),
        P(("blk", "grp"), None),
    )
    out_specs = (P(("blk", "grp"), None), P(("blk", "grp"), None), P(), P())
    return jax.shard_map(
        per_device, mesh=mesh, in_specs=in_specs, out_specs=out_specs, check_vma=False
    )
```

```python
import math

import jax
import jax.numpy as jnp
from jax import lax
from jax.experimental import pallas as pl
from jax.experimental.pallas import tpu as pltpu
from jax.sharding import PartitionSpec as P

BF16 = jnp.bfloat16
F32 = jnp.float32
GROUP = 24
MIB = 1 << 20
SMEM = pl.BlockSpec(memory_space=pltpu.SMEM)
VMEM = pl.BlockSpec(memory_space=pltpu.VMEM)
ANY = pl.BlockSpec(memory_space=pl.ANY)
KERNEL_VMEM = 24 * MIB
COST = pl.CostEstimate(flops=1024, bytes_accessed=1024, transcendentals=0)
SLAB_STEPS = (((1, True), (3, True), (2, True), (0, False)), ((1, False), (3, False), (2, False)))
CLASS_ORDER = (2, 1, 3, 0)

RING = 8


def along_grp(x, where):
    def target(i):
        z, y, c = where(i // 4, i // 2 % 2, i % 2)
        return z % RING * 4 + y * 2 + c

    return lax.ppermute(x, "grp", [(i, target(i)) for i in range(4 * RING)])


def other_core(x):
    return along_grp(x, lambda z, y, c: (z, y, 1 - c))


def other_y(x):
    return along_grp(x, lambda z, y, c: (z, 1 - y, c))


def along_z(x, distance):
    return along_grp(x, lambda z, y, c: (z + distance, y, c))


def two_along_z(x):
    return along_grp(x, lambda z, y, c: (z + 2 - z % 2 * 4, y, c))


def flip_z(x, bit):
    return along_grp(x, lambda z, y, c: (z ^ bit, y, c))


def along_blk(x, distance):
    n = lax.axis_size("blk")
    return lax.ppermute(x, "blk", [(i, (i + distance) % n) for i in range(n)])


def flip_blk(x, bit):
    n = lax.axis_size("blk")
    return lax.ppermute(x, "blk", [(i, i ^ bit) for i in range(n)])


def chunk_of(me, order, same_y, same_core):
    z, y, c = me // 4, me // 2 % 2, me % 2
    z = lax.rem(z + order + RING, RING)
    y = y if same_y else 1 - y
    c = c if same_core else 1 - c
    return z * 4 + y * 2 + c


def placed(block, col, live):
    zero = jnp.zeros_like(block)
    left = jnp.where(jnp.logical_and(live, col == 0), block, zero)
    right = jnp.where(jnp.logical_and(live, col == 1), block, zero)
    return left, right


def slab_lists(lists, pos_ref, counts_ref, blocks_ref, feats, acc):
    for k, feat_ref in zip(lists, feats, strict=True):
        live = counts_ref[k]
        feat = feat_ref[...]

        def step(s, _, k=k, live=live, feat=feat):
            rows, places = [], []
            for u in range(GROUP):
                j = s * GROUP + u
                p = pos_ref[k, j]
                left, right = placed(blocks_ref[k, j], p % 2, j < live)
                rows.append(jnp.concatenate([left, right], axis=1))
                places.append(p // 2)
            products = jnp.dot(jnp.concatenate(rows, axis=0), feat, preferred_element_type=F32)
            tile = rows[0].shape[0]
            for u in range(GROUP):
                acc[places[u]] += products[u * tile : (u + 1) * tile]
            return 0

        lax.fori_loop(0, (live + GROUP - 1) // GROUP, step, 0)


def list_of(blk, source):
    behind, same = source
    y = blk % 2
    return (2 * behind + (0 if same else 2 * y - 1) + 8) % 8


def slab_sums(me, sources, block_pos, counts, blocks, feats, acc=None):
    _, slots, tile, _ = blocks.shape
    rows, width = feats[0].shape
    shape = jax.ShapeDtypeStruct((4 * RING * rows // tile, tile, width), F32)

    def kernel(me_ref, pos_ref, counts_ref, blocks_ref, *refs):
        out = refs[-1]
        lists = [list_of(me_ref[1], source) for source in sources]
        if acc is None:

            def clear(i, _):
                out[i] = jnp.zeros(out.shape[1:], F32)
                return 0

            lax.fori_loop(0, out.shape[0], clear, 0)
        slab_lists(lists, pos_ref, counts_ref, blocks_ref, refs[: len(sources)], out)

    more = [] if acc is None else [acc]
    return pl.pallas_call(
        kernel,
        out_shape=shape,
        in_specs=[SMEM, SMEM, SMEM, VMEM] + [VMEM] * (len(feats) + len(more)),
        out_specs=VMEM,
        input_output_aliases={4 + len(feats): 0} if more else {},
        compiler_params=pltpu.CompilerParams(vmem_limit_bytes=KERNEL_VMEM),
        cost_estimate=COST,
        name="slab_sums",
    )(me, block_pos, counts, blocks, *feats, *more)


FAR_Y = ((3, False), (-3, False), (4, False))
NEAR = ((1, True), (1, False), (-1, True), (-1, False), (2, False), (-2, False))
REST = ((3, True), (-3, True), (4, True), (2, True), (-2, True), (0, False), (0, True))


def slab_parts(me, sources, block_pos, counts, blocks, feats, acc):
    _, slots, tile, _ = blocks.shape
    rows, width = feats[0].shape
    groups = (FAR_Y, NEAR, REST)

    def kernel(me_ref, pos_ref, counts_ref, blocks_ref, *refs):
        total, outs = refs[len(sources)], refs[len(sources) + 1 :]
        lists = [list_of(me_ref[1], source) for source in sources]
        slab_lists(lists, pos_ref, counts_ref, blocks_ref, refs[: len(sources)], total)
        mine = me_ref[0]
        for out, (same_core, group) in zip(
            outs, [(same, group) for same in (False, True) for group in groups], strict=True
        ):
            for i, (order, same_y) in enumerate(group):
                chunk = chunk_of(mine, order, same_y, same_core)
                for half in range(2):
                    start = (2 * i + half) * tile
                    out[start : start + tile, :] = total[chunk * 2 + half].astype(BF16)

    return pl.pallas_call(
        kernel,
        out_shape=[
            jax.ShapeDtypeStruct((len(group) * rows, width), BF16) for group in groups * 2
        ],
        in_specs=[SMEM, SMEM, SMEM, VMEM] + [VMEM] * (len(feats) + 1),
        out_specs=[VMEM] * 6,
        compiler_params=pltpu.CompilerParams(vmem_limit_bytes=KERNEL_VMEM),
        cost_estimate=COST,
        name="slab_parts",
    )(me, block_pos, counts, blocks, *feats, acc)


def mid_kernel(refs_in, refs_out):
    me_ref, feats, cotangent, degree, w_self, w_neigh, parts = refs_in
    out, grad_slab, grad_self, mine, theirs = refs_out
    deg = degree[...]
    summed = parts[0][...].astype(F32)
    for part in parts[1:]:
        summed = summed + part[...].astype(F32)
    mean = (summed / deg).astype(BF16)
    x, ws, wn = feats[...], w_self[...], w_neigh[...]
    pre = jnp.dot(x, ws, preferred_element_type=F32) + jnp.dot(mean, wn, preferred_element_type=F32)
    sigma = jax.nn.sigmoid(pre)
    out[...] = (pre * sigma).astype(BF16)
    grad = (cotangent[...].astype(F32) * sigma * (1.0 + pre * (1.0 - sigma))).astype(BF16)
    transposed = (((1,), (1,)), ((), ()))
    back = lax.dot_general(grad, wn, transposed, preferred_element_type=F32)
    grad_slab[...] = (back / deg).astype(BF16)
    grad_self[...] = lax.dot_general(grad, ws, transposed, preferred_element_type=F32)
    over_rows = (((0,), (0,)), ((), ()))
    local_self = lax.dot_general(x, grad, over_rows, preferred_element_type=F32).astype(BF16)
    local_neigh = lax.dot_general(mean, grad, over_rows, preferred_element_type=F32).astype(BF16)
    first = me_ref[0] % 2 == 0
    mine[...] = jnp.where(first, local_self, local_neigh)
    theirs[...] = jnp.where(first, local_neigh, local_self)


def middle(me, feats, cotangent, degree, w_self, w_neigh, parts):
    rows, width = feats.shape

    def kernel(*refs):
        mid_kernel((*refs[:6], refs[6 : 6 + len(parts)]), refs[6 + len(parts) :])

    low, wide = jax.ShapeDtypeStruct((rows, width), BF16), jax.ShapeDtypeStruct((rows, width), F32)
    square = jax.ShapeDtypeStruct((width, width), BF16)
    return pl.pallas_call(
        kernel,
        out_shape=(low, low, wide, square, square),
        in_specs=[SMEM] + [VMEM] * (5 + len(parts)),
        out_specs=(VMEM,) * 5,
        compiler_params=pltpu.CompilerParams(vmem_limit_bytes=16 * MIB),
        cost_estimate=COST,
        name="middle",
    )(me, feats, cotangent, degree, w_self, w_neigh, *parts)


def put(grads, chunk, value):
    tile = grads.shape[1]
    for half in range(2):
        grads[chunk * 2 + half] = value[half * tile : (half + 1) * tile]


def gathered(me, rows, pieces, after=()):
    width, tile = pieces[0][0].shape[1], rows // 2

    def kernel(me_ref, *refs):
        mine, out = me_ref[0], refs[-1]
        for ref, (_, places) in zip(refs[: len(pieces)], pieces, strict=True):
            for i, place in enumerate(places):
                put(out, chunk_of(mine, *place), ref[i * rows : (i + 1) * rows, :])

    return pl.pallas_call(
        kernel,
        out_shape=jax.ShapeDtypeStruct((4 * RING * 2, tile, width), BF16),
        in_specs=[SMEM] + [VMEM] * len(pieces) + [ANY] * len(after),
        out_specs=VMEM,
        compiler_params=pltpu.CompilerParams(vmem_limit_bytes=KERNEL_VMEM),
        cost_estimate=COST,
        name="gathered",
    )(me, *[array for array, _ in pieces], *after)


def packed(arrays, after=()):
    starts = [0]
    for array in arrays:
        starts.append(starts[-1] + array.shape[0])

    def kernel(*refs):
        for ref, start, end in zip(refs[: len(arrays)], starts[:-1], starts[1:], strict=True):
            refs[-1][start:end, :] = ref[...]

    return pl.pallas_call(
        kernel,
        out_shape=jax.ShapeDtypeStruct((starts[-1], arrays[0].shape[1]), BF16),
        in_specs=[VMEM] * len(arrays) + [ANY] * len(after),
        out_specs=VMEM,
        compiler_params=pltpu.CompilerParams(vmem_limit_bytes=KERNEL_VMEM),
        cost_estimate=COST,
        name="packed",
    )(*arrays, *after)


def class_list(k, pos_ref, counts_ref, blocks_ref, grads, out):
    live = counts_ref[k]

    def step(s, total):
        cols, picked = [], []
        for u in range(GROUP):
            j = s * GROUP + u
            p = pos_ref[k, j]
            top, bottom = placed(blocks_ref[k, j].T, p % 2, j < live)
            cols.append(jnp.concatenate([top, bottom], axis=0))
            picked.append(grads[p // 2])
        return total + jnp.dot(
            jnp.concatenate(cols, axis=1),
            jnp.concatenate(picked, axis=0),
            preferred_element_type=F32,
        )

    out[...] = lax.fori_loop(
        0, (live + GROUP - 1) // GROUP, step, jnp.zeros(out.shape, F32)
    ).astype(out.dtype)


def class_sums(me, block_pos, counts, blocks, grads, last):
    _, slots, tile, _ = blocks.shape
    width = grads.shape[2]
    rows = 2 * tile

    def kernel(me_ref, pos_ref, counts_ref, blocks_ref, _, last_ref, grads_ref, *outs):
        for i, place in enumerate(last[1]):
            put(grads_ref, chunk_of(me_ref[0], *place), last_ref[i * rows : (i + 1) * rows, :])
        for behind, out in zip(CLASS_ORDER, outs, strict=True):
            for i, same in enumerate((True, False)):
                k = list_of(me_ref[1], (behind, same))
                view = out.at[pl.ds(i * rows, rows), :]
                class_list(k, pos_ref, counts_ref, blocks_ref, grads_ref, view)

    pair = jax.ShapeDtypeStruct((2 * rows, width), BF16)
    return pl.pallas_call(
        kernel,
        out_shape=[jax.ShapeDtypeStruct(grads.shape, BF16)] + [pair] * len(CLASS_ORDER),
        in_specs=[SMEM, SMEM, SMEM] + [VMEM] * 3,
        out_specs=[VMEM] * (1 + len(CLASS_ORDER)),
        input_output_aliases={4: 0},
        compiler_params=pltpu.CompilerParams(vmem_limit_bytes=KERNEL_VMEM),
        cost_estimate=COST,
        name="class_sums",
    )(me, block_pos, counts, blocks, grads, last[0])[1:]


def wide_sum(*terms):
    total = terms[0].astype(F32)
    for term in terms[1:]:
        total = total + term.astype(F32)
    return total


def sums(outs, after=(), me=None):
    arrays = []
    for terms in outs:
        for array, *_ in terms:
            if not any(array is other for other in arrays):
                arrays.append(array)

    def find(array):
        return next(i for i, other in enumerate(arrays) if other is array)

    scalars = [] if me is None else [me]

    def kernel(*refs):
        me_refs, refs = refs[: len(scalars)], refs[len(scalars) :]
        for out, terms in zip(refs[len(arrays) + len(after) :], outs, strict=True):
            total = None
            for array, first, count, *parity in terms:
                term = refs[find(array)][first : first + count, :].astype(F32)
                if parity:
                    mine = me_refs[0][0] // 4 % 2 == parity[0]
                    term = jnp.where(mine, term, jnp.zeros_like(term))
                total = term if total is None else total + term
            out[...] = total.astype(BF16)

    width = arrays[0].shape[1]
    return pl.pallas_call(
        kernel,
        out_shape=[jax.ShapeDtypeStruct((terms[0][2], width), BF16) for terms in outs],
        in_specs=[SMEM] * len(scalars) + [VMEM] * len(arrays) + [ANY] * len(after),
        out_specs=[VMEM] * len(outs),
        compiler_params=pltpu.CompilerParams(vmem_limit_bytes=KERNEL_VMEM),
        cost_estimate=COST,
        name="sums",
    )(*scalars, *arrays, *after)


def pair_sum(first, second, after=()):
    rows = first.shape[0]
    return sums([[(first, 0, rows), (second, 0, rows)]], after)[0]


def slab_reduced(me, rows, sent, kept):
    def at(array, first, count=1):
        return array[first * rows : (first + count) * rows]

    def both(first, count, *arrays):
        return [(array, first * rows, count * rows) for array in arrays]

    far_y = other_y(pair_sum(kept[0], other_core(sent[0])))
    near, more = kept[1], other_core(sent[1])
    ahead, behind, mid = sums([both(first, 2, near, more) for first in (0, 2, 4)])
    from_behind, from_ahead = along_z(ahead, 1), along_z(behind, -1)
    mid_y = other_y(mid)
    rest, more = kept[2], other_core(sent[2])
    ahead, behind, opposite = sums(
        [both(i, 1, rest, more, far_y) for i in range(3)], [from_behind, from_ahead]
    )
    three_ahead, three_behind = along_z(ahead, 1), along_z(behind, -1)
    opposite = two_along_z(opposite)
    one = (0, rows)
    two_ahead, two_behind = sums(
        [
            [*both(3, 1, rest, more), *both(0, 1, mid_y), (three_ahead, *one), (opposite, *one, 0)],
            [*both(4, 1, rest, more), *both(1, 1, mid_y), (three_behind, *one), (opposite, *one, 1)],
        ],
        me=me,
    )
    from_two_behind, from_two_ahead = along_z(two_ahead, 2), along_z(two_behind, -2)
    own_y = other_y(
        sums([both(5, 1, rest, more) + both(1, 1, from_behind, from_ahead)], [three_ahead])[0]
    )
    base = wide_sum(at(rest, 6), at(more, 6), at(from_behind, 0), at(from_ahead, 0))
    return [base, own_y, from_two_behind, from_two_ahead]


def slab_gathered(me, even, own, mine, theirs):
    behind2, ahead2 = along_z(own, 2), along_z(own, -2)
    own_y = other_y(own)
    behind3, ahead3 = along_z(behind2, 1), along_z(ahead2, -1)
    opposite = two_along_z(jnp.where(even, behind2, ahead2))
    total = pair_sum(mine, other_core(packed([theirs], [own_y])), [behind2, ahead2])
    mid_y = other_y(packed([behind2, ahead2], [total]))
    total = pair_sum(total, flip_blk(total, 2), [behind3, ahead3])
    far = packed([behind3, ahead3, opposite], [mid_y, total])
    far_y = other_y(far)
    total = pair_sum(total, flip_blk(total, 4), [far])
    both = packed([own, own_y], [total])
    from_behind, from_ahead = along_z(both, 1), along_z(both, -1)
    total = pair_sum(total, flip_blk(total, 1), [from_behind, from_ahead])
    half = packed(
        [own, own_y, behind2, ahead2, mid_y, far, far_y, from_behind, from_ahead], [total]
    )
    half_core = other_core(half)
    places = (
        (0, True), (0, False), (-2, True), (2, True), (-2, False), (2, False), (-3, True), (3, True), (4, True),
        (-3, False), (3, False), (4, False), (-1, True), (-1, False), (1, True), (1, False),
    )

    def on(places, same_core):
        return [(*place, same_core) for place in places]

    grads = gathered(me, own.shape[0], [(half, on(places, True))])
    return grads, (half_core, on(places, False)), total


def weight_sums(place, total, pair):
    total = pair_sum(total, flip_z(total, 4), [pair])
    total = pair_sum(total, flip_z(total, 2))
    total = pair_sum(total, flip_z(total, 1))
    total = pair_sum(total, other_y(total))
    twin = other_core(total)
    first = place % 2 == 0
    return jnp.where(first, total, twin).astype(F32), jnp.where(first, twin, total).astype(F32)


def per_device(features, blocks, block_pos, counts, degree, w_self, w_neigh, cotangent):
    cycle_size = lax.axis_size("blk")
    group_size = lax.axis_size("grp")
    rows, width = features.shape
    place = lax.axis_index("grp").astype(jnp.int32)
    me = jnp.stack([place, lax.axis_index("blk").astype(jnp.int32)])
    even = place // 4 % 2 == 0
    table = (block_pos[0, 0], counts[0, 0], blocks[0, 0])

    feats = {(0, True): features, (0, False): flip_blk(features, 1)}
    for same in (True, False):
        for behind in (1, 3, 2):
            feats[behind, same] = along_blk(feats[0, same], 2 * behind)
    acc = slab_sums(me, [(0, True)], *table, [features])
    for sources in SLAB_STEPS[:-1]:
        acc = slab_sums(me, sources, *table, [feats[source] for source in sources], acc)
    sources = SLAB_STEPS[-1]
    shares = slab_parts(me, sources, *table, [feats[source] for source in sources], acc)
    parts = slab_reduced(me, rows, shares[:3], shares[3:])
    scale_deg = degree.astype(F32)[:, None]
    out, grad_slab, grad_self, mine, theirs = middle(
        me, features, cotangent, scale_deg, w_self, w_neigh, parts
    )

    grads, last, total = slab_gathered(me, even, grad_slab, mine, theirs)
    pairs = class_sums(me, *table, grads, last)
    arrived = [along_blk(pair, -2 * x) for pair, x in zip(pairs[:-1], CLASS_ORDER[:-1], strict=True)]
    arrived.append(pairs[-1])
    other = sums([[(pair, rows, rows) for pair in arrived]])[0]
    back_sum = wide_sum(grad_self, flip_blk(other, 1), *[pair[:rows] for pair in arrived])
    grad_x = back_sum.astype(BF16)

    total_self, total_neigh = weight_sums(place, total, pairs[0])
    norm_scale = 1.0 / math.sqrt(rows * cycle_size * group_size)
    return (out, grad_x, total_self * norm_scale, total_neigh * norm_scale)


def solution(mesh):
    in_specs = (
        P(("blk", "grp"), None),
        P("blk", "grp", None, None, None, None),
        P("blk", "grp", None, None),
        P("blk", "grp", None),
        P(("blk", "grp")),
        P(),
        P(),
        P(("blk", "grp"), None),
    )
    out_specs = (P(("blk", "grp"), None), P(("blk", "grp"), None), P(), P())
    return jax.shard_map(
        per_device, mesh=mesh, in_specs=in_specs, out_specs=out_specs, check_vma=False
    )
```

```python
import math

import jax
import jax.numpy as jnp
from jax import lax
from jax.experimental import pallas as pl
from jax.experimental.pallas import tpu as pltpu
from jax.sharding import PartitionSpec as P

BF16 = jnp.bfloat16
F32 = jnp.float32
GROUP = 24
MIB = 1 << 20
SMEM = pl.BlockSpec(memory_space=pltpu.SMEM)
VMEM = pl.BlockSpec(memory_space=pltpu.VMEM)
ANY = pl.BlockSpec(memory_space=pl.ANY)
KERNEL_VMEM = 24 * MIB
COST = pl.CostEstimate(flops=1024, bytes_accessed=1024, transcendentals=0)
SLAB_STEPS = (((1, True), (3, True), (2, True), (0, False)), ((1, False), (3, False), (2, False)))
CLASS_ORDER = (2, 1, 3, 0)

RING = 8


def along_grp(x, where):
    def target(i):
        z, y, c = where(i // 4, i // 2 % 2, i % 2)
        return z % RING * 4 + y * 2 + c

    return lax.ppermute(x, "grp", [(i, target(i)) for i in range(4 * RING)])


def other_core(x):
    return along_grp(x, lambda z, y, c: (z, y, 1 - c))


def other_y(x):
    return along_grp(x, lambda z, y, c: (z, 1 - y, c))


def along_z(x, distance):
    return along_grp(x, lambda z, y, c: (z + distance, y, c))


def two_along_z(x):
    return along_grp(x, lambda z, y, c: (z + 2 - z % 2 * 4, y, c))


def flip_z(x, bit):
    return along_grp(x, lambda z, y, c: (z ^ bit, y, c))


def along_blk(x, distance):
    n = lax.axis_size("blk")
    return lax.ppermute(x, "blk", [(i, (i + distance) % n) for i in range(n)])


def flip_blk(x, bit):
    n = lax.axis_size("blk")
    return lax.ppermute(x, "blk", [(i, i ^ bit) for i in range(n)])


def chunk_of(me, order, same_y, same_core):
    z, y, c = me // 4, me // 2 % 2, me % 2
    z = lax.rem(z + order + RING, RING)
    y = y if same_y else 1 - y
    c = c if same_core else 1 - c
    return z * 4 + y * 2 + c


def placed(block, col, live):
    zero = jnp.zeros_like(block)
    left = jnp.where(jnp.logical_and(live, col == 0), block, zero)
    right = jnp.where(jnp.logical_and(live, col == 1), block, zero)
    return left, right


def slab_lists(lists, pos_ref, counts_ref, blocks_ref, feats, acc):
    for k, feat_ref in zip(lists, feats, strict=True):
        live = counts_ref[k]
        feat = feat_ref[...]

        def step(s, _, k=k, live=live, feat=feat):
            rows, places = [], []
            for u in range(GROUP):
                j = s * GROUP + u
                p = pos_ref[k, j]
                left, right = placed(blocks_ref[k, j], p % 2, j < live)
                rows.append(jnp.concatenate([left, right], axis=1))
                places.append(p // 2)
            products = jnp.dot(jnp.concatenate(rows, axis=0), feat, preferred_element_type=F32)
            tile = rows[0].shape[0]
            for u in range(GROUP):
                acc[places[u]] += products[u * tile : (u + 1) * tile]
            return 0

        lax.fori_loop(0, (live + GROUP - 1) // GROUP, step, 0)


def list_of(blk, source):
    behind, same = source
    y = blk % 2
    return (2 * behind + (0 if same else 2 * y - 1) + 8) % 8


def slab_sums(me, sources, block_pos, counts, blocks, feats, acc=None):
    _, slots, tile, _ = blocks.shape
    rows, width = feats[0].shape
    shape = jax.ShapeDtypeStruct((4 * RING * rows // tile, tile, width), F32)

    def kernel(me_ref, pos_ref, counts_ref, blocks_ref, *refs):
        out = refs[-1]
        lists = [list_of(me_ref[1], source) for source in sources]
        if acc is None:

            def clear(i, _):
                out[i] = jnp.zeros(out.shape[1:], F32)
                return 0

            lax.fori_loop(0, out.shape[0], clear, 0)
        slab_lists(lists, pos_ref, counts_ref, blocks_ref, refs[: len(sources)], out)

    more = [] if acc is None else [acc]
    return pl.pallas_call(
        kernel,
        out_shape=shape,
        in_specs=[SMEM, SMEM, SMEM, VMEM] + [VMEM] * (len(feats) + len(more)),
        out_specs=VMEM,
        input_output_aliases={4 + len(feats): 0} if more else {},
        compiler_params=pltpu.CompilerParams(vmem_limit_bytes=KERNEL_VMEM),
        cost_estimate=COST,
        name="slab_sums",
    )(me, block_pos, counts, blocks, *feats, *more)


FAR_Y = ((3, False), (-3, False), (4, False))
NEAR = ((1, True), (1, False), (-1, True), (-1, False), (2, False), (-2, False))
REST = ((3, True), (-3, True), (4, True), (2, True), (-2, True), (0, False), (0, True))


def slab_parts(me, sources, block_pos, counts, blocks, feats, acc):
    _, slots, tile, _ = blocks.shape
    rows, width = feats[0].shape
    groups = (FAR_Y, NEAR, REST)

    def kernel(me_ref, pos_ref, counts_ref, blocks_ref, *refs):
        total, outs = refs[len(sources)], refs[len(sources) + 1 :]
        lists = [list_of(me_ref[1], source) for source in sources]
        slab_lists(lists, pos_ref, counts_ref, blocks_ref, refs[: len(sources)], total)
        mine = me_ref[0]
        for out, (same_core, group) in zip(
            outs, [(same, group) for same in (False, True) for group in groups], strict=True
        ):
            for i, (order, same_y) in enumerate(group):
                chunk = chunk_of(mine, order, same_y, same_core)
                for half in range(2):
                    start = (2 * i + half) * tile
                    out[start : start + tile, :] = total[chunk * 2 + half].astype(BF16)

    return pl.pallas_call(
        kernel,
        out_shape=[
            jax.ShapeDtypeStruct((len(group) * rows, width), BF16) for group in groups * 2
        ],
        in_specs=[SMEM, SMEM, SMEM, VMEM] + [VMEM] * (len(feats) + 1),
        out_specs=[VMEM] * 6,
        compiler_params=pltpu.CompilerParams(vmem_limit_bytes=KERNEL_VMEM),
        cost_estimate=COST,
        name="slab_parts",
    )(me, block_pos, counts, blocks, *feats, acc)


def mid_kernel(refs_in, refs_out):
    me_ref, feats, cotangent, degree, w_self, w_neigh, parts = refs_in
    out, grad_slab, grad_self, mine, theirs = refs_out
    deg = degree[...]
    summed = parts[0][...].astype(F32)
    for part in parts[1:]:
        summed = summed + part[...].astype(F32)
    mean = (summed / deg).astype(BF16)
    x, ws, wn = feats[...], w_self[...], w_neigh[...]
    pre = jnp.dot(x, ws, preferred_element_type=F32) + jnp.dot(mean, wn, preferred_element_type=F32)
    sigma = jax.nn.sigmoid(pre)
    out[...] = (pre * sigma).astype(BF16)
    grad = (cotangent[...].astype(F32) * sigma * (1.0 + pre * (1.0 - sigma))).astype(BF16)
    transposed = (((1,), (1,)), ((), ()))
    back = lax.dot_general(grad, wn, transposed, preferred_element_type=F32)
    grad_slab[...] = (back / deg).astype(BF16)
    grad_self[...] = lax.dot_general(grad, ws, transposed, preferred_element_type=F32)
    over_rows = (((0,), (0,)), ((), ()))
    local_self = lax.dot_general(x, grad, over_rows, preferred_element_type=F32).astype(BF16)
    local_neigh = lax.dot_general(mean, grad, over_rows, preferred_element_type=F32).astype(BF16)
    first = me_ref[0] % 2 == 0
    mine[...] = jnp.where(first, local_self, local_neigh)
    theirs[...] = jnp.where(first, local_neigh, local_self)


def middle(me, feats, cotangent, degree, w_self, w_neigh, parts):
    rows, width = feats.shape

    def kernel(*refs):
        mid_kernel((*refs[:6], refs[6 : 6 + len(parts)]), refs[6 + len(parts) :])

    low, wide = jax.ShapeDtypeStruct((rows, width), BF16), jax.ShapeDtypeStruct((rows, width), F32)
    square = jax.ShapeDtypeStruct((width, width), BF16)
    return pl.pallas_call(
        kernel,
        out_shape=(low, low, wide, square, square),
        in_specs=[SMEM] + [VMEM] * (5 + len(parts)),
        out_specs=(VMEM,) * 5,
        compiler_params=pltpu.CompilerParams(vmem_limit_bytes=16 * MIB),
        cost_estimate=COST,
        name="middle",
    )(me, feats, cotangent, degree, w_self, w_neigh, *parts)


def put(grads, chunk, value):
    tile = grads.shape[1]
    for half in range(2):
        grads[chunk * 2 + half] = value[half * tile : (half + 1) * tile]


def gathered(me, rows, pieces, after=()):
    width, tile = pieces[0][0].shape[1], rows // 2

    def kernel(me_ref, *refs):
        mine, out = me_ref[0], refs[-1]
        for ref, (_, places) in zip(refs[: len(pieces)], pieces, strict=True):
            for i, place in enumerate(places):
                put(out, chunk_of(mine, *place), ref[i * rows : (i + 1) * rows, :])

    return pl.pallas_call(
        kernel,
        out_shape=jax.ShapeDtypeStruct((4 * RING * 2, tile, width), BF16),
        in_specs=[SMEM] + [VMEM] * len(pieces) + [ANY] * len(after),
        out_specs=VMEM,
        compiler_params=pltpu.CompilerParams(vmem_limit_bytes=KERNEL_VMEM),
        cost_estimate=COST,
        name="gathered",
    )(me, *[array for array, _ in pieces], *after)


def packed(arrays, after=()):
    starts = [0]
    for array in arrays:
        starts.append(starts[-1] + array.shape[0])

    def kernel(*refs):
        for ref, start, end in zip(refs[: len(arrays)], starts[:-1], starts[1:], strict=True):
            refs[-1][start:end, :] = ref[...]

    return pl.pallas_call(
        kernel,
        out_shape=jax.ShapeDtypeStruct((starts[-1], arrays[0].shape[1]), BF16),
        in_specs=[VMEM] * len(arrays) + [ANY] * len(after),
        out_specs=VMEM,
        compiler_params=pltpu.CompilerParams(vmem_limit_bytes=KERNEL_VMEM),
        cost_estimate=COST,
        name="packed",
    )(*arrays, *after)


def class_list(k, pos_ref, counts_ref, blocks_ref, grads, out):
    live = counts_ref[k]

    def step(s, total):
        cols, picked = [], []
        for u in range(GROUP):
            j = s * GROUP + u
            p = pos_ref[k, j]
            top, bottom = placed(blocks_ref[k, j].T, p % 2, j < live)
            cols.append(jnp.concatenate([top, bottom], axis=0))
            picked.append(grads[p // 2])
        return total + jnp.dot(
            jnp.concatenate(cols, axis=1),
            jnp.concatenate(picked, axis=0),
            preferred_element_type=F32,
        )

    out[...] = lax.fori_loop(
        0, (live + GROUP - 1) // GROUP, step, jnp.zeros(out.shape, F32)
    ).astype(out.dtype)


def class_sums(me, block_pos, counts, blocks, grads, last):
    _, slots, tile, _ = blocks.shape
    width = grads.shape[2]
    rows = 2 * tile

    def kernel(me_ref, pos_ref, counts_ref, blocks_ref, _, last_ref, grads_ref, *outs):
        for i, place in enumerate(last[1]):
            put(grads_ref, chunk_of(me_ref[0], *place), last_ref[i * rows : (i + 1) * rows, :])
        for behind, out in zip(CLASS_ORDER, outs, strict=True):
            for i, same in enumerate((True, False)):
                k = list_of(me_ref[1], (behind, same))
                view = out.at[pl.ds(i * rows, rows), :]
                class_list(k, pos_ref, counts_ref, blocks_ref, grads_ref, view)

    pair = jax.ShapeDtypeStruct((2 * rows, width), BF16)
    return pl.pallas_call(
        kernel,
        out_shape=[jax.ShapeDtypeStruct(grads.shape, BF16)] + [pair] * len(CLASS_ORDER),
        in_specs=[SMEM, SMEM, SMEM] + [VMEM] * 3,
        out_specs=[VMEM] * (1 + len(CLASS_ORDER)),
        input_output_aliases={4: 0},
        compiler_params=pltpu.CompilerParams(vmem_limit_bytes=KERNEL_VMEM),
        cost_estimate=COST,
        name="class_sums",
    )(me, block_pos, counts, blocks, grads, last[0])[1:]


def wide_sum(*terms):
    total = terms[0].astype(F32)
    for term in terms[1:]:
        total = total + term.astype(F32)
    return total


def sums(outs, after=(), me=None):
    arrays = []
    for terms in outs:
        for array, *_ in terms:
            if not any(array is other for other in arrays):
                arrays.append(array)

    def find(array):
        return next(i for i, other in enumerate(arrays) if other is array)

    scalars = [] if me is None else [me]

    def kernel(*refs):
        me_refs, refs = refs[: len(scalars)], refs[len(scalars) :]
        for out, terms in zip(refs[len(arrays) + len(after) :], outs, strict=True):
            total = None
            for array, first, count, *parity in terms:
                term = refs[find(array)][first : first + count, :].astype(F32)
                if parity:
                    mine = me_refs[0][0] // 4 % 2 == parity[0]
                    term = jnp.where(mine, term, jnp.zeros_like(term))
                total = term if total is None else total + term
            out[...] = total.astype(BF16)

    width = arrays[0].shape[1]
    return pl.pallas_call(
        kernel,
        out_shape=[jax.ShapeDtypeStruct((terms[0][2], width), BF16) for terms in outs],
        in_specs=[SMEM] * len(scalars) + [VMEM] * len(arrays) + [ANY] * len(after),
        out_specs=[VMEM] * len(outs),
        compiler_params=pltpu.CompilerParams(vmem_limit_bytes=KERNEL_VMEM),
        cost_estimate=COST,
        name="sums",
    )(*scalars, *arrays, *after)


def pair_sum(first, second, after=()):
    rows = first.shape[0]
    return sums([[(first, 0, rows), (second, 0, rows)]], after)[0]


def slab_reduced(me, rows, sent, kept):
    def at(array, first, count=1):
        return array[first * rows : (first + count) * rows]

    def both(first, count, *arrays):
        return [(array, first * rows, count * rows) for array in arrays]

    far_y = other_y(pair_sum(kept[0], other_core(sent[0])))
    near, more = kept[1], other_core(sent[1])
    ahead, behind, mid = sums([both(first, 2, near, more) for first in (0, 2, 4)])
    from_behind, from_ahead = along_z(ahead, 1), along_z(behind, -1)
    mid_y = other_y(mid)
    rest, more = kept[2], other_core(sent[2])
    ahead, behind, opposite = sums(
        [both(i, 1, rest, more, far_y) for i in range(3)], [from_behind, from_ahead]
    )
    three_ahead, three_behind = along_z(ahead, 1), along_z(behind, -1)
    opposite = two_along_z(opposite)
    one = (0, rows)
    two_ahead, two_behind = sums(
        [
            [*both(3, 1, rest, more), *both(0, 1, mid_y), (three_ahead, *one), (opposite, *one, 0)],
            [*both(4, 1, rest, more), *both(1, 1, mid_y), (three_behind, *one), (opposite, *one, 1)],
        ],
        me=me,
    )
    from_two_behind, from_two_ahead = along_z(two_ahead, 2), along_z(two_behind, -2)
    own_y = other_y(
        sums([both(5, 1, rest, more) + both(1, 1, from_behind, from_ahead)], [three_ahead])[0]
    )
    base = wide_sum(at(rest, 6), at(more, 6), at(from_behind, 0), at(from_ahead, 0))
    return [base, own_y, from_two_behind, from_two_ahead]


def slab_gathered(me, even, own, mine, theirs):
    behind2, ahead2 = along_z(own, 2), along_z(own, -2)
    own_y = other_y(own)
    behind3, ahead3 = along_z(behind2, 1), along_z(ahead2, -1)
    opposite = two_along_z(jnp.where(even, behind2, ahead2))
    total = pair_sum(mine, other_core(packed([theirs], [own_y])), [behind2, ahead2])
    mid_y = other_y(packed([behind2, ahead2]))
    total = pair_sum(total, flip_blk(total, 2), [behind3, ahead3])
    far = packed([behind3, ahead3, opposite], [mid_y, total])
    far_y = other_y(far)
    total = pair_sum(total, flip_blk(total, 4), [far])
    both = packed([own, own_y], [total])
    from_behind, from_ahead = along_z(both, 1), along_z(both, -1)
    total = pair_sum(total, flip_blk(total, 1), [from_behind, from_ahead])
    half = packed(
        [own, own_y, behind2, ahead2, mid_y, far, far_y, from_behind, from_ahead], [total]
    )
    half_core = other_core(half)
    places = (
        (0, True), (0, False), (-2, True), (2, True), (-2, False), (2, False), (-3, True), (3, True), (4, True),
        (-3, False), (3, False), (4, False), (-1, True), (-1, False), (1, True), (1, False),
    )

    def on(places, same_core):
        return [(*place, same_core) for place in places]

    grads = gathered(me, own.shape[0], [(half, on(places, True))])
    return grads, (half_core, on(places, False)), total


def weight_sums(place, total, pair):
    total = pair_sum(total, flip_z(total, 4), [pair])
    total = pair_sum(total, flip_z(total, 2))
    total = pair_sum(total, flip_z(total, 1))
    total = pair_sum(total, other_y(total))
    twin = other_core(total)
    first = place % 2 == 0
    return jnp.where(first, total, twin).astype(F32), jnp.where(first, twin, total).astype(F32)


def per_device(features, blocks, block_pos, counts, degree, w_self, w_neigh, cotangent):
    cycle_size = lax.axis_size("blk")
    group_size = lax.axis_size("grp")
    rows, width = features.shape
    place = lax.axis_index("grp").astype(jnp.int32)
    me = jnp.stack([place, lax.axis_index("blk").astype(jnp.int32)])
    even = place // 4 % 2 == 0
    table = (block_pos[0, 0], counts[0, 0], blocks[0, 0])

    feats = {(0, True): features, (0, False): flip_blk(features, 1)}
    for same in (True, False):
        for behind in (1, 3, 2):
            feats[behind, same] = along_blk(feats[0, same], 2 * behind)
    acc = slab_sums(me, [(0, True)], *table, [features])
    for sources in SLAB_STEPS[:-1]:
        acc = slab_sums(me, sources, *table, [feats[source] for source in sources], acc)
    sources = SLAB_STEPS[-1]
    shares = slab_parts(me, sources, *table, [feats[source] for source in sources], acc)
    parts = slab_reduced(me, rows, shares[:3], shares[3:])
    scale_deg = degree.astype(F32)[:, None]
    out, grad_slab, grad_self, mine, theirs = middle(
        me, features, cotangent, scale_deg, w_self, w_neigh, parts
    )

    grads, last, total = slab_gathered(me, even, grad_slab, mine, theirs)
    pairs = class_sums(me, *table, grads, last)
    arrived = [along_blk(pair, -2 * x) for pair, x in zip(pairs[:-1], CLASS_ORDER[:-1], strict=True)]
    arrived.append(pairs[-1])
    other = sums([[(pair, rows, rows) for pair in arrived]])[0]
    back_sum = wide_sum(grad_self, flip_blk(other, 1), *[pair[:rows] for pair in arrived])
    grad_x = back_sum.astype(BF16)

    total_self, total_neigh = weight_sums(place, total, pairs[0])
    norm_scale = 1.0 / math.sqrt(rows * cycle_size * group_size)
    return (out, grad_x, total_self * norm_scale, total_neigh * norm_scale)


def solution(mesh):
    in_specs = (
        P(("blk", "grp"), None),
        P("blk", "grp", None, None, None, None),
        P("blk", "grp", None, None),
        P("blk", "grp", None),
        P(("blk", "grp")),
        P(),
        P(),
        P(("blk", "grp"), None),
    )
    out_specs = (P(("blk", "grp"), None), P(("blk", "grp"), None), P(), P())
    return jax.shard_map(
        per_device, mesh=mesh, in_specs=in_specs, out_specs=out_specs, check_vma=False
    )
```
